128 devices in a mesh: dp: 32 (over x, z, core), mp: 4 (over y).
Axes of the slice: x: 4, y: 4, z: 4, core: 2. Of those that a mesh axis runs over, the one named last changes fastest.
Arguments:
- embedding: bfloat16 [8192, 7168], P('dp', 'mp'), may hold values from -6 to 6
- hidden: bfloat16 [8192, 7168], P('dp', 'mp'), may hold values from -6 to 6
- embed_gain: float32 [7168], P('mp'), may hold values from 0.3 to 1.7
- hidden_gain: float32 [7168], P('mp'), may hold values from 0.3 to 1.7
- cotangent: bfloat16 [8192, 4096], P('dp', 'mp'), may hold values from -0.015625 to 0.015625
- left_stat: float32 [32768, 4096], P('dp', 'mp'), may hold values from -6 to 6
- right_stat: float32 [32768, 4096], P('dp', 'mp'), may hold values from -6 to 6
- left_root: bfloat16 [32768, 4096], P('dp', 'mp')
- right_root: bfloat16 [32768, 4096], P('dp', 'mp')
- owners: int32 [4, 14], replicated, may hold values from 0 to 31, as said below
Outputs:
- left_new: float32 [32768, 4096], P('dp', 'mp')
- right_new: float32 [32768, 4096], P('dp', 'mp')
- update: bfloat16 [4, 1024, 14336], P('mp', 'dp')
The draws below stay inside these ranges and needn't reach their ends.
Inputs may be any that keep to these rules, and one draw needn't show every extreme that they name: In each block column the 14 owners are all different.
All inputs are finite; a program needn't handle non-finite values.
Results may differ from the reference program's by a relative error of at most 0.023.
Values may be sent and summed in bfloat16 or wider, within the bound.
A program may use at most 192 MiB of HBM per device.

```python
import jax
import jax.numpy as jnp
from jax import lax

D = 7168
BLOCK = 1024
TOK_DEV = 256
TOKENS = 8192
DIN = 14336
DOUT = 4096
BROWS = 14
N_DP = 32
N_MP = 4


def root_matrix(key, spread):
    total_rows = N_DP * BLOCK
    total_cols = N_MP * BLOCK
    rows = jnp.arange(total_rows, dtype=jnp.int32) % BLOCK
    cols = jnp.arange(total_cols, dtype=jnp.int32) % BLOCK
    diagonal = (rows[:, None] == cols[None, :]).astype(jnp.float32)
    noise = jax.random.normal(key, (total_rows, total_cols), jnp.float32)
    return (diagonal + noise * (spread / BLOCK ** 0.5)).astype(jnp.bfloat16)


def draw_left_root(key, part):
    key = jax.random.fold_in(key, 11)
    return root_matrix(key, 0.6)


def draw_right_root(key, part):
    key = jax.random.fold_in(key, 12)
    return root_matrix(key, 0.6)


def draw_owners(key, part):
    key = jax.random.fold_in(key, 13)
    keys = jax.random.split(key, N_MP + 1)
    picks = jax.vmap(lambda k: jax.random.permutation(k, jnp.arange(N_DP, dtype=jnp.int32)))(keys[:N_MP])
    picks = picks[:, :BROWS].astype(jnp.int32)
    middle = 1 + jax.random.permutation(keys[N_MP], jnp.arange(N_DP - 2, dtype=jnp.int32))[:BROWS - 2]
    first = jnp.concatenate([jnp.array([0, N_DP - 1], dtype=jnp.int32), middle.astype(jnp.int32)])
    order = jax.random.permutation(jax.random.fold_in(keys[N_MP], 1), jnp.arange(BROWS, dtype=jnp.int32))
    first = first[order]
    return picks.at[0].set(first).astype(jnp.int32)


def steps_of(stream_key, extent, pieces, least, top_value):
    def one(axis_at, blocks):
        draws = jax.random.uniform(jax.random.fold_in(jax.random.fold_in(stream_key, 6), axis_at), (blocks,), jnp.float32, least / len(pieces), top_value / len(pieces))
        return jnp.repeat(jnp.exp(draws), extent[axis_at] // blocks).reshape((-1,) + (1,) * (len(extent) - axis_at - 1))

    level = one(*pieces[0])
    for cut in pieces[1:]:
        level = level * one(*cut)
    return level


def normal_values(rng, dims, width, most, shards=(), kind=jnp.bfloat16):
    factor_of = steps_of(rng, dims, shards, -0.22, 0.18) if shards else 1.0
    values = jax.random.normal(rng, dims, jnp.float32) * width * factor_of
    return jnp.minimum(jnp.maximum(values, -most), most).astype(kind)


def setup_inputs(seed: int = 0) -> dict:
    arg_keys = jax.random.split(jax.random.key(seed), 11)
    return {
        "embedding": normal_values(arg_keys[0], (TOKENS, D), 1.0, 6.0, ((0, 32), (1, 4))),
        "hidden": normal_values(arg_keys[1], (TOKENS, D), 1.0, 6.0, ((0, 32), (1, 4))),
        "embed_gain": jnp.clip(0.3 + 1.40000004 * jax.random.uniform(arg_keys[2], (D,), jnp.float32) ** steps_of(arg_keys[2], (D,), ((0, 4),), -0.2, 0.2), 0.3, 1.7),
        "hidden_gain": jnp.clip(0.3 + 1.40000004 * jax.random.uniform(arg_keys[3], (D,), jnp.float32) ** steps_of(arg_keys[3], (D,), ((0, 4),), -0.2, 0.2), 0.3, 1.7),
        "cotangent": normal_values(arg_keys[4], (TOKENS, DOUT), (TOKENS * 16) ** -0.5, 0.015625, ((0, 32), (1, 4))),
        "left_stat": normal_values(arg_keys[5], (N_DP * BLOCK, DOUT), 1.0, 6.0, ((0, 32), (1, 4)), jnp.float32),
        "right_stat": normal_values(arg_keys[6], (N_DP * BLOCK, DOUT), 1.0, 6.0, ((0, 32), (1, 4)), jnp.float32),
        "left_root": draw_left_root(jax.random.fold_in(arg_keys[10], 71), 0),
        "right_root": draw_right_root(jax.random.fold_in(arg_keys[10], 71), 0),
        "owners": draw_owners(jax.random.fold_in(arg_keys[10], 71), 0),
    }


def rms_norm(values_in, gain):
    values = values_in.astype(jnp.float32)
    scale = lax.rsqrt(lax.optimization_barrier(jnp.mean(values * values, axis=1)) + 1e-06)
    return (values * scale[:, None] * gain[None, :]).astype(jnp.bfloat16)

def reference(embedding, hidden, embed_gain, hidden_gain, cotangent, left_stat, right_stat, left_root, right_root, owners):
    normed = jnp.concatenate([rms_norm(embedding, embed_gain), rms_norm(hidden, hidden_gain)], axis=1)
    normed_groups = normed.reshape(N_DP, TOK_DEV, DIN)
    cot_groups = cotangent.reshape(N_DP, TOK_DEV, DOUT)

    def add_group(total, pair):
        left_part, right_part = pair
        partial_value = jnp.dot(left_part.T, right_part, preferred_element_type=jnp.float32).astype(jnp.bfloat16)
        partial_value = lax.optimization_barrier(partial_value)
        return (total + partial_value.astype(jnp.float32), None)
    summed, unused = lax.scan(add_group, jnp.zeros((DIN, DOUT), jnp.float32), (normed_groups, cot_groups))
    gradient = summed.astype(jnp.bfloat16)
    left_four = left_stat.reshape(N_DP, BLOCK, N_MP, BLOCK)
    right_four = right_stat.reshape(N_DP, BLOCK, N_MP, BLOCK)
    lroot_four = left_root.reshape(N_DP, BLOCK, N_MP, BLOCK)
    rroot_four = right_root.reshape(N_DP, BLOCK, N_MP, BLOCK)

    def one_block(items):
        block, old_left, old_right, root_left, root_right = items
        gram_left = lax.dot_general(block, block, (((1,), (1,)), ((), ())), preferred_element_type=jnp.float32)
        gram_right = lax.dot_general(block, block, (((0,), (0,)), ((), ())), preferred_element_type=jnp.float32)
        inner = jnp.dot(block, root_right, preferred_element_type=jnp.float32).astype(jnp.bfloat16)
        result = jnp.dot(root_left, inner, preferred_element_type=jnp.float32).astype(jnp.bfloat16)
        return (0.9 * old_left + 0.1 * gram_left, 0.9 * old_right + 0.1 * gram_right, result)
    columns_out = []
    for column in range(N_MP):
        col_owner = owners[column].astype(jnp.int32)
        blocks = gradient[:, column * BLOCK:(column + 1) * BLOCK].reshape(BROWS, BLOCK, BLOCK)
        old_left = jnp.take(left_four[:, :, column, :], col_owner, axis=0)
        old_right = jnp.take(right_four[:, :, column, :], col_owner, axis=0)
        root_left = jnp.take(lroot_four[:, :, column, :], col_owner, axis=0)
        root_right = jnp.take(rroot_four[:, :, column, :], col_owner, axis=0)
        new_left, new_right, results = lax.map(one_block, (blocks, old_left, old_right, root_left, root_right))
        left_four = left_four.at[col_owner, :, column, :].set(new_left)
        right_four = right_four.at[col_owner, :, column, :].set(new_right)
        columns_out.append(jnp.transpose(results, (2, 0, 1)).reshape(BLOCK, DIN))
    update = jnp.stack(columns_out, axis=0)
    return (left_four.reshape(N_DP * BLOCK, DOUT), right_four.reshape(N_DP * BLOCK, DOUT), update)
```

```python
import functools

import jax
import jax.numpy as jnp
from jax import lax
from jax.experimental import pallas as pl
from jax.experimental.pallas import tpu as pltpu
from jax.sharding import PartitionSpec as P

MESH = pl.DeviceIdType.MESH
F32 = jnp.float32
BF16 = jnp.bfloat16
WIDTH = 7168
PART = 1792
HALF = 896
DELTAS = (0, 1, 3, 2)


def coords():
    dp = lax.axis_index("dp")
    return dp // 8, lax.axis_index("mp"), (dp // 2) % 4, dp % 2


def device(x, y, z, core):
    return ((x * 4 + z) * 2 + core, y)


def remote(src, dst, send, recv, dest):
    return pltpu.make_async_remote_copy(
        src_ref=src, dst_ref=dst, send_sem=send, recv_sem=recv, device_id=dest, device_id_type=MESH
    )


def row_squares(ref):
    acc = jnp.zeros((256, 128), F32)
    for i in range(PART // 128):
        v = ref[:, i * 128 : (i + 1) * 128].astype(F32)
        acc = acc + v * v
    return jnp.sum(jnp.transpose(acc), axis=0, keepdims=True)


def reduce_kernel(
    emb, hid, eg, hg, cot, share,
    ct, nb, sq, sc, part, r1, q, r2, yb, sh,
    sq_s, sq_r, sib_s, sib_r, ct_s, ct_r, rel_s, rel_r, p1_s, p1_r, p2_s, p2_r, y_s, y_r, loc,
):
    x, y, z, core = coords()
    sib = device(x, y, z, 1 - core)
    nbr = {
        "x": (device((x + 1) % 4, y, z, core), device((x + 3) % 4, y, z, core), x),
        "z": (device(x, y, (z + 1) % 4, core), device(x, y, (z + 3) % 4, core), z),
    }
    barrier = pltpu.get_barrier_semaphore()
    peers = [sib]
    for axis in ("x", "z"):
        peers += [nbr[axis][0], nbr[axis][1]]
    for d in (1, 2, 3):
        peers += [device(x, (y + d) % 4, z, core), device(x, (y + d) % 4, z, 1 - core)]
    for peer in peers:
        pl.semaphore_signal(barrier, inc=1, device_id=peer, device_id_type=MESH)

    ct[0, core] = jnp.transpose(cot[...]).reshape(4, 4, 64, 256)
    sq[0] = jnp.concatenate([row_squares(emb), row_squares(hid), jnp.zeros((6, 256), F32)], axis=0)
    pl.semaphore_wait(barrier, len(peers))

    sends = []

    def go(cp):
        cp.start()
        sends.append(cp)
        return cp

    sq_cp = [
        go(remote(sq.at[0], sq.at[i], sq_s.at[i - 1], sq_r.at[i - 1], device(x, (y + i) % 4, z, core)))
        for i in (1, 2, 3)
    ]
    ct_cp = {}
    rel_cp = {}
    rel_cp[0] = go(remote(ct.at[0, core], ct.at[0, core], rel_s.at[0], rel_r.at[0], sib))
    for s in (1, 2, 3):
        ct_cp[s] = go(
            remote(ct.at[0, core], ct.at[s, core], ct_s.at[s - 1], ct_r.at[s - 1],
                   device(x, (y + 4 - DELTAS[s]) % 4, z, core))
        )
    n_cp = remote(emb, nb.at[core], sib_s.at[0], sib_r.at[0], sib)
    l_cp = pltpu.make_async_copy(emb, nb.at[core], loc.at[0])

    @pl.when(core == 0)
    def _():
        remote(hid, nb.at[core], sib_s.at[0], sib_r.at[0], sib).start()
        pltpu.make_async_copy(emb, nb.at[core], loc.at[0]).start()

    @pl.when(core == 1)
    def _():
        remote(emb, nb.at[core], sib_s.at[0], sib_r.at[0], sib).start()
        pltpu.make_async_copy(hid, nb.at[core], loc.at[0]).start()

    sends.append(n_cp)
    gain = jnp.where(core == 0, eg[...], hg[...])
    for cp in sq_cp:
        cp.wait_recv()
    sc[core] = lax.rsqrt((sq[0] + sq[1] + sq[2] + sq[3]) / WIDTH + 1e-6)
    sc_cp = go(remote(sc.at[core], sc.at[core], sib_s.at[1], sib_r.at[1], sib))
    l_cp.wait()
    n_cp.wait_recv()
    sc_cp.wait_recv()
    rel_cp[0].wait_recv()
    scale = [jnp.where(core == 0, sc[t, 0:1], sc[t, 1:2]) for t in (0, 1)]

    def relay(s):
        ct_cp[s].wait_recv()
        rel_cp[s] = go(remote(ct.at[s, core], ct.at[s, core], rel_s.at[s], rel_r.at[s], sib))

    axes = (("x", "z"), ("z", "x"))
    cps = {}

    def product(s):
        if s > 0:
            rel_cp[s].wait_recv()

        @pl.loop(0, 4)
        def _(g):
            xg = lax.rem(x + g, 4)
            zg = lax.rem(z + g, 4)

            def lhs(t, ab):
                v = ct[s, t, xg] if ab == 0 else ct[s, t, :, zg]
                return (v.reshape(256, 256).astype(F32) * scale[t]).astype(BF16)

            for ab, at in ((0, xg), (1, zg)):
                lanes = slice(ab * HALF, (ab + 1) * HALF)
                acc = jnp.dot(lhs(0, ab), nb[0, :, lanes], preferred_element_type=F32)
                acc = acc + jnp.dot(lhs(1, ab), nb[1, :, lanes], preferred_element_type=F32)
                part[ab, s, at] = acc.astype(BF16).reshape(4, 64, HALF)

    def ring1(ab, s):
        plus, minus, pos = nbr[axes[ab][0]]
        p1, m1, m2 = (pos + 1) % 4, (pos + 3) % 4, (pos + 2) % 4
        src = part.at[ab, s]

        def cp(i, ref, dest):
            return remote(ref, r1.at[ab, s, i], p1_s.at[ab, s, i], p1_r.at[ab, s, i], dest)

        return [
            cp(0, src.at[m2, 0:2], plus),
            cp(1, src.at[m2, 2:4], minus),
            cp(2, src.at[p1, 2:4], plus),
            cp(3, src.at[m1, 0:2], minus),
            cp(4, src.at[p1, 0:2], plus),
            cp(5, src.at[m1, 2:4], minus),
        ], (pos, p1, m1)

    def ring2(ab, s):
        plus, minus, pos = nbr[axes[ab][1]]
        p1, m1, m2 = (pos + 1) % 4, (pos + 3) % 4, (pos + 2) % 4
        src = q.at[ab, s]

        def cp(i, ref, dest):
            return remote(ref, r2.at[ab, s, i], p2_s.at[ab, s, i], p2_r.at[ab, s, i], dest)

        return [
            cp(0, src.at[m2, 0:32], plus),
            cp(1, src.at[m2, 32:64], minus),
            cp(2, src.at[p1, 32:64], plus),
            cp(3, src.at[m1, 0:32], minus),
            cp(4, src.at[p1, 0:32], plus),
            cp(5, src.at[m1, 32:64], minus),
        ], (pos, p1, m1)

    def add(a, *rest):
        out = a.astype(F32)
        for r in rest:
            out = out + r.astype(F32)
        return out

    def stage_a(s):
        product(s)
        if s < 3:
            relay(s + 1)
        for ab in (0, 1):
            cps[1, ab, s] = ring1(ab, s)
            for i in range(4):
                go(cps[1, ab, s][0][i])

    def stage_b(s):
        for ab in (0, 1):
            c, (pos, p1, m1) = cps[1, ab, s]
            c[0].wait_recv()
            part[ab, s, p1, 0:2] = add(part[ab, s, p1, 0:2], r1[ab, s, 0]).astype(BF16)
            go(c[4])
            c[1].wait_recv()
            part[ab, s, m1, 2:4] = add(part[ab, s, m1, 2:4], r1[ab, s, 1]).astype(BF16)
            go(c[5])

    def stage_c(s):
        for ab in (0, 1):
            c, (pos, p1, m1) = cps[1, ab, s]
            for i in (2, 3, 4, 5):
                c[i].wait_recv()
            q[ab, s, 0:2] = add(part[ab, s, pos, 0:2], r1[ab, s, 4], r1[ab, s, 3]).astype(BF16)
            q[ab, s, 2:4] = add(part[ab, s, pos, 2:4], r1[ab, s, 2], r1[ab, s, 5]).astype(BF16)
            cps[2, ab, s] = ring2(ab, s)
            for i in range(4):
                go(cps[2, ab, s][0][i])

    def stage_d(s):
        for ab in (0, 1):
            c, (pos, p1, m1) = cps[2, ab, s]
            c[0].wait_recv()
            q[ab, s, p1, 0:32] = add(q[ab, s, p1, 0:32], r2[ab, s, 0]).astype(BF16)
            go(c[4])
            c[1].wait_recv()
            q[ab, s, m1, 32:64] = add(q[ab, s, m1, 32:64], r2[ab, s, 1]).astype(BF16)
            go(c[5])

    y_cp = []

    def stage_e(s):
        for ab in (0, 1):
            c, (pos, p1, m1) = cps[2, ab, s]
            for i in (2, 3, 4, 5):
                c[i].wait_recv()
            lanes = slice(ab * HALF, (ab + 1) * HALF)
            g = gain[:, lanes]
            yb[s, 0, :, lanes] = (add(q[ab, s, pos, 0:32], r2[ab, s, 4], r2[ab, s, 3]) * g).astype(BF16)
            yb[s, 1, :, lanes] = (add(q[ab, s, pos, 32:64], r2[ab, s, 2], r2[ab, s, 5]) * g).astype(BF16)
        for rel in (0, 1):
            to = (core + rel) % 2
            if s == 0 and rel == 0:
                cp = pltpu.make_async_copy(yb.at[s, to], sh.at[core * 4 + y], loc.at[1])
                cp.start()
            else:
                cp = go(
                    remote(yb.at[s, to], sh.at[core * 4 + y], y_s.at[s, rel], y_r.at[s, rel],
                           device(x, (y + DELTAS[s]) % 4, z, to))
                )
            y_cp.append(cp)

    stages = {"a": stage_a, "b": stage_b, "c": stage_c, "d": stage_d, "e": stage_e}
    for turn in range(8):
        for behind, name in enumerate("abcde"):
            if 0 <= turn - behind < 4:
                stages[name](turn - behind)
    for i, cp in enumerate(y_cp):
        if i == 0:
            cp.wait()
        else:
            cp.wait_recv()
    for i in range(8):
        share[:, i * PART : (i + 1) * PART] = sh[i]
    for cp in sends:
        cp.wait_send()


def reduced_share(emb, hid, eg, hg, cot):
    dma = pltpu.SemaphoreType.DMA
    return pl.pallas_call(
        reduce_kernel,
        out_shape=jax.ShapeDtypeStruct((32, 2 * WIDTH), BF16),
        in_specs=[pl.BlockSpec(memory_space=pltpu.VMEM)] * 5,
        out_specs=pl.BlockSpec(memory_space=pltpu.VMEM),
        scratch_shapes=[
            pltpu.VMEM((4, 2, 4, 4, 64, 256), BF16),
            pltpu.VMEM((2, 256, PART), BF16),
            pltpu.VMEM((4, 8, 256), F32),
            pltpu.VMEM((2, 8, 256), F32),
            pltpu.VMEM((2, 4, 4, 4, 64, HALF), BF16),
            pltpu.VMEM((2, 4, 6, 2, 64, HALF), BF16),
            pltpu.VMEM((2, 4, 4, 64, HALF), BF16),
            pltpu.VMEM((2, 4, 6, 32, HALF), BF16),
            pltpu.VMEM((4, 2, 32, PART), BF16),
            pltpu.VMEM((8, 32, PART), BF16),
            dma((3,)), dma((3,)), dma((2,)), dma((2,)), dma((3,)), dma((3,)), dma((4,)), dma((4,)),
            dma((2, 4, 6)), dma((2, 4, 6)), dma((2, 4, 6)), dma((2, 4, 6)), dma((4, 2)), dma((4, 2)), dma((2,)),
        ],
        compiler_params=pltpu.CompilerParams(
            collective_id=0, has_side_effects=True, vmem_limit_bytes=60 * 2**20
        ),
        name="reduce_share",
    )(emb, hid, eg, hg, cot)


def body(
    embedding,
    hidden,
    embed_gain,
    hidden_gain,
    cotangent,
    left_stat,
    right_stat,
    left_root,
    right_root,
    owners,
):
    share = reduced_share(embedding, hidden, embed_gain[None], hidden_gain[None], cotangent)
    total_in = share.shape[1]
    replicas = lax.axis_size("dp")
    side = cotangent.shape[1]
    sliver = side // replicas
    block_rows = total_in // side
    my_replica = lax.axis_index("dp")
    my_column = lax.axis_index("mp")
    column_owners = lax.dynamic_index_in_dim(owners, my_column, 0, keepdims=False)
    owner_hot = (column_owners[None, :] == jnp.arange(replicas, dtype=jnp.int32)[:, None]).astype(
        jnp.bfloat16
    )
    pieces = share.reshape(sliver, block_rows, side)
    outgoing = jnp.einsum(
        "or,srb->osb", owner_hot, pieces, preferred_element_type=jnp.float32
    ).astype(jnp.bfloat16)
    arrived = lax.all_to_all(outgoing, "dp", split_axis=0, concat_axis=1, tiled=True)
    grad_t = arrived.reshape(side, side)
    owned = jnp.any(column_owners == my_replica)
    gram_left = lax.dot_general(
        grad_t, grad_t, (((0,), (0,)), ((), ())), preferred_element_type=jnp.float32
    )
    gram_right = lax.dot_general(
        grad_t, grad_t, (((1,), (1,)), ((), ())), preferred_element_type=jnp.float32
    )
    left_new = jnp.where(owned, 0.9 * left_stat + 0.1 * gram_left, left_stat)
    right_new = jnp.where(owned, 0.9 * right_stat + 0.1 * gram_right, right_stat)
    inner_t = lax.dot_general(
        right_root, grad_t, (((0,), (0,)), ((), ())), preferred_element_type=jnp.float32
    ).astype(jnp.bfloat16)
    result_t = lax.dot_general(
        inner_t, left_root, (((1,), (1,)), ((), ())), preferred_element_type=jnp.float32
    ).astype(jnp.bfloat16)
    returned = lax.all_to_all(
        result_t.reshape(replicas, sliver, side), "dp", split_axis=0, concat_axis=0, tiled=True
    )
    placed = jnp.einsum(
        "or,osb->srb", owner_hot, returned, preferred_element_type=jnp.float32
    ).astype(jnp.bfloat16)
    update = placed.reshape(1, sliver, total_in)
    return (left_new, right_new, update)


def solution(mesh):
    placed = (
        P("dp", "mp"),
        P("dp", "mp"),
        P("mp"),
        P("mp"),
        P("dp", "mp"),
        P("dp", "mp"),
        P("dp", "mp"),
        P("dp", "mp"),
        P("dp", "mp"),
        P(),
    )
    return jax.shard_map(
        body,
        mesh=mesh,
        in_specs=placed,
        out_specs=(P("dp", "mp"), P("dp", "mp"), P("mp", "dp", None)),
        check_vma=False,
    )
```

```python
import functools

import jax
import jax.numpy as jnp
from jax import lax
from jax.experimental import pallas as pl
from jax.experimental.pallas import tpu as pltpu
from jax.sharding import PartitionSpec as P

MESH = pl.DeviceIdType.MESH
F32 = jnp.float32
BF16 = jnp.bfloat16
WIDTH = 7168
PART = 1792
HALF = 896
DELTAS = (0, 1, 3, 2)


def coords():
    dp = lax.axis_index("dp")
    return dp // 8, lax.axis_index("mp"), (dp // 2) % 4, dp % 2


def device(x, y, z, core):
    return ((x * 4 + z) * 2 + core, y)


def remote(src, dst, send, recv, dest):
    return pltpu.make_async_remote_copy(
        src_ref=src, dst_ref=dst, send_sem=send, recv_sem=recv, device_id=dest, device_id_type=MESH
    )


def row_squares(ref):
    acc = jnp.zeros((256, 128), F32)
    for i in range(PART // 128):
        v = ref[:, i * 128 : (i + 1) * 128].astype(F32)
        acc = acc + v * v
    return jnp.sum(jnp.transpose(acc), axis=0, keepdims=True)


def reduce_kernel(
    emb, hid, eg, hg, cot, own, lstat, rstat, lroot, rroot, lnew, rnew, update,
    ct, nb, sq, sc, part, r1, r2, yb, sh, blocks, outb, arr, ret, tb, rt, lt, st, so,
    sq_s, sq_r, sib_s, sib_r, ct_s, ct_r, rel_s, rel_r, p1_s, p1_r, p2_s, p2_r, y_s, y_r, loc,
    o_s, o_r, b_s, b_r, st_i, st_o,
):
    x, y, z, core = coords()
    sib = device(x, y, z, 1 - core)
    nbr = {
        "x": (device((x + 1) % 4, y, z, core), device((x + 3) % 4, y, z, core), x),
        "z": (device(x, y, (z + 1) % 4, core), device(x, y, (z + 3) % 4, core), z),
    }
    barrier = pltpu.get_barrier_semaphore()
    me = (x * 4 + z) * 2 + core

    def peer_of(k):
        tx, tz, tc = (x + k // 8) % 4, (z + (k // 2) % 4) % 4, (core + k % 2) % 2
        return (tx * 4 + tz) * 2 + tc

    for d in (1, 2, 3):
        for c in (core, 1 - core):
            pl.semaphore_signal(barrier, inc=1, device_id=device(x, (y + d) % 4, z, c), device_id_type=MESH)

    @pl.loop(1, 32)
    def _(k):
        pl.semaphore_signal(barrier, inc=1, device_id=(peer_of(k), y), device_id_type=MESH)

    r_cp = pltpu.make_async_copy(rroot, tb, loc.at[2])
    r_cp.start()

    ct[0, core] = jnp.transpose(cot[...]).reshape(4, 4, 64, 256)
    sq[0] = jnp.concatenate([row_squares(emb), row_squares(hid), jnp.zeros((6, 256), F32)], axis=0)
    pl.semaphore_wait(barrier, 37)

    sends = []

    def go(cp):
        cp.start()
        sends.append(cp)
        return cp

    sq_cp = [
        go(remote(sq.at[0], sq.at[i], sq_s.at[i - 1], sq_r.at[i - 1], device(x, (y + i) % 4, z, core)))
        for i in (1, 2, 3)
    ]
    ct_cp = {}
    rel_cp = {}
    rel_cp[0] = go(remote(ct.at[0, core], ct.at[0, core], rel_s.at[0], rel_r.at[0], sib))
    for s in (1, 2, 3):
        ct_cp[s] = go(
            remote(ct.at[0, core], ct.at[s, core], ct_s.at[s - 1], ct_r.at[s - 1],
                   device(x, (y + 4 - DELTAS[s]) % 4, z, core))
        )
    n_cp = remote(emb, nb.at[core], sib_s.at[0], sib_r.at[0], sib)
    l_cp = pltpu.make_async_copy(emb, nb.at[core], loc.at[0])

    @pl.when(core == 0)
    def _():
        remote(hid, nb.at[core], sib_s.at[0], sib_r.at[0], sib).start()
        pltpu.make_async_copy(emb, nb.at[core], loc.at[0]).start()

    @pl.when(core == 1)
    def _():
        remote(emb, nb.at[core], sib_s.at[0], sib_r.at[0], sib).start()
        pltpu.make_async_copy(hid, nb.at[core], loc.at[0]).start()

    sends.append(n_cp)
    gain = jnp.where(core == 0, eg[...], hg[...])
    for cp in sq_cp:
        cp.wait_recv()
    sc[core] = lax.rsqrt((sq[0] + sq[1] + sq[2] + sq[3]) / WIDTH + 1e-6)
    sc_cp = go(remote(sc.at[core], sc.at[core], sib_s.at[1], sib_r.at[1], sib))
    l_cp.wait()
    n_cp.wait_recv()
    sc_cp.wait_recv()
    rel_cp[0].wait_recv()
    scale = [jnp.where(core == 0, sc[t, 0:1], sc[t, 1:2]) for t in (0, 1)]

    def relay(s):
        ct_cp[s].wait_recv()
        rel_cp[s] = go(remote(ct.at[s, core], ct.at[s, core], rel_s.at[s], rel_r.at[s], sib))

    axes = (("x", "z"), ("z", "x"))
    cps = {}

    def product(s):
        if s > 0:
            rel_cp[s].wait_recv()

        @pl.loop(0, 4)
        def _(g):
            xg = lax.rem(x + g, 4)
            zg = lax.rem(z + g, 4)

            def lhs(t, ab):
                v = ct[s, t, xg] if ab == 0 else ct[s, t, :, zg]
                return (v.reshape(256, 256).astype(F32) * scale[t]).astype(BF16)

            for ab, at in ((0, xg), (1, zg)):
                lanes = slice(ab * HALF, (ab + 1) * HALF)
                acc = jnp.dot(lhs(0, ab), nb[0, :, lanes], preferred_element_type=F32)
                acc = acc + jnp.dot(lhs(1, ab), nb[1, :, lanes], preferred_element_type=F32)
                part[ab, s, at] = acc.astype(BF16).reshape(4, 64, HALF)

    def ring1(ab, s):
        plus, minus, pos = nbr[axes[ab][0]]
        p1, m1, m2 = (pos + 1) % 4, (pos + 3) % 4, (pos + 2) % 4
        src = part.at[ab, s]

        def cp(i, ref, dest):
            return remote(ref, r1.at[ab, s, i], p1_s.at[ab, s, i], p1_r.at[ab, s, i], dest)

        return [
            cp(0, src.at[m2, 0:2], plus),
            cp(1, src.at[m2, 2:4], minus),
            cp(2, src.at[p1, 2:4], plus),
            cp(3, src.at[m1, 0:2], minus),
            cp(4, src.at[p1, 0:2], plus),
            cp(5, src.at[m1, 2:4], minus),
        ], (pos, p1, m1)

    def ring2(ab, s):
        plus, minus, pos = nbr[axes[ab][1]]
        p1, m1, m2 = (pos + 1) % 4, (pos + 3) % 4, (pos + 2) % 4
        src = part.at[ab, s, nbr[axes[ab][0]][2]]

        def cp(i, ref, dest):
            return remote(ref, r2.at[ab, s, i], p2_s.at[ab, s, i], p2_r.at[ab, s, i], dest)

        return [
            cp(0, src.at[m2, 0:32], plus),
            cp(1, src.at[m2, 32:64], minus),
            cp(2, src.at[p1, 32:64], plus),
            cp(3, src.at[m1, 0:32], minus),
            cp(4, src.at[p1, 0:32], plus),
            cp(5, src.at[m1, 32:64], minus),
        ], (pos, p1, m1)

    def add(a, *rest):
        out = a.astype(F32)
        for r in rest:
            out = out + r.astype(F32)
        return out

    def stage_a(s):
        product(s)
        if s < 3:
            relay(s + 1)
        for ab in (0, 1):
            cps[1, ab, s] = ring1(ab, s)
            for i in range(4):
                go(cps[1, ab, s][0][i])

    def stage_b(s):
        for ab in (0, 1):
            c, (pos, p1, m1) = cps[1, ab, s]
            c[0].wait_recv()
            part[ab, s, p1, 0:2] = add(part[ab, s, p1, 0:2], r1[ab, s, 0]).astype(BF16)
            go(c[4])
            c[1].wait_recv()
            part[ab, s, m1, 2:4] = add(part[ab, s, m1, 2:4], r1[ab, s, 1]).astype(BF16)
            go(c[5])

    def stage_c(s):
        for ab in (0, 1):
            c, (pos, p1, m1) = cps[1, ab, s]
            for i in (2, 3, 4, 5):
                c[i].wait_recv()
            part[ab, s, pos, 0:2] = add(part[ab, s, pos, 0:2], r1[ab, s, 4], r1[ab, s, 3]).astype(BF16)
            part[ab, s, pos, 2:4] = add(part[ab, s, pos, 2:4], r1[ab, s, 2], r1[ab, s, 5]).astype(BF16)
            cps[2, ab, s] = ring2(ab, s)
            for i in range(4):
                go(cps[2, ab, s][0][i])

    def stage_d(s):
        for ab in (0, 1):
            c, (pos, p1, m1) = cps[2, ab, s]
            c[0].wait_recv()
            o = nbr[axes[ab][0]][2]
            part[ab, s, o, p1, 0:32] = add(part[ab, s, o, p1, 0:32], r2[ab, s, 0]).astype(BF16)
            go(c[4])
            c[1].wait_recv()
            part[ab, s, o, m1, 32:64] = add(part[ab, s, o, m1, 32:64], r2[ab, s, 1]).astype(BF16)
            go(c[5])

    y_cp = []

    def stage_e(s):
        for ab in (0, 1):
            c, (pos, p1, m1) = cps[2, ab, s]
            for i in (2, 3, 4, 5):
                c[i].wait_recv()
            lanes = slice(ab * HALF, (ab + 1) * HALF)
            g = gain[:, lanes]
            o = nbr[axes[ab][0]][2]
            yb[s, 0, :, lanes] = (add(part[ab, s, o, pos, 0:32], r2[ab, s, 4], r2[ab, s, 3]) * g).astype(BF16)
            yb[s, 1, :, lanes] = (add(part[ab, s, o, pos, 32:64], r2[ab, s, 2], r2[ab, s, 5]) * g).astype(BF16)
        for rel in (0, 1):
            to = (core + rel) % 2
            if s == 0 and rel == 0:
                cp = pltpu.make_async_copy(yb.at[s, to], sh.at[core * 4 + y], loc.at[1])
                cp.start()
            else:
                cp = go(
                    remote(yb.at[s, to], sh.at[core * 4 + y], y_s.at[s, rel], y_r.at[s, rel],
                           device(x, (y + DELTAS[s]) % 4, z, to))
                )
            y_cp.append(cp)

    stages = {"a": stage_a, "b": stage_b, "c": stage_c, "d": stage_d, "e": stage_e}
    def transpose_root(out):
        @pl.loop(0, 8)
        def _(i):
            at = pl.ds(pl.multiple_of(i * 128, 128), 128)
            out[at, :] = jnp.transpose(tb[:, at])

    def stat_in(i, side):
        rows = pl.ds(pl.multiple_of(i * 256, 256), 256)
        return pltpu.make_async_copy((lstat, rstat)[side].at[rows], st.at[side], st_i.at[side])

    def stat_out(i, side):
        rows = pl.ds(pl.multiple_of(i * 256, 256), 256)
        return pltpu.make_async_copy(so.at[side], (lnew, rnew)[side].at[rows], st_o.at[side])

    for turn in range(8):
        for behind, name in enumerate("abcde"):
            if 0 <= turn - behind < 4:
                stages[name](turn - behind)
        if turn == 3:
            r_cp.wait()
            transpose_root(rt)
            l_root = pltpu.make_async_copy(lroot, tb, loc.at[3])
            l_root.start()
        if turn == 4:
            l_root.wait()
            transpose_root(lt)
            stat_in(0, 0).start()
            stat_in(0, 1).start()
    for i, cp in enumerate(y_cp):
        if i == 0:
            cp.wait()
        else:
            cp.wait_recv()

    for r in range(14):
        at = r * 1024
        done = 0
        while done < 1024:
            i, lane = (at + done) // PART, (at + done) % PART
            size = min(1024 - done, PART - lane)
            blocks[r, :, done : done + size] = sh[i, :, lane : lane + size]
            done += size

    owner_of = [own[y, r] for r in range(14)]

    def row_of(d):
        row = jnp.int32(0)
        for r in range(14):
            row = jnp.where(owner_of[r] == d, jnp.int32(r), row)
        return row

    def to_owner(k):
        t = peer_of(k)
        return t, remote(outb.at[t], arr.at[me], o_s.at[k], o_r.at[k], (t, y))

    def back(k):
        t = peer_of(k)
        return t, remote(outb.at[t], ret.at[me], b_s.at[k], b_r.at[k], (t, y))

    @pl.loop(1, 32)
    def _(k):
        t, cp = to_owner(k)
        outb[t] = blocks[row_of(t)]
        cp.start()

    arr[me] = blocks[row_of(me)]
    mine = jnp.int32(0)
    for r in range(14):
        mine = jnp.where(owner_of[r] == me, jnp.int32(1), mine)
    for cp in sends:
        cp.wait_send()

    @pl.loop(1, 32)
    def _(k):
        _, cp = to_owner(k)
        cp.wait()

    @pl.loop(0, 4)
    def _(i):
        g = lax.rem(i + 1, 4)
        tx = lax.rem(x + g, 4)
        rows = pl.ds(pl.multiple_of(tx * 256, 256), 256)
        inner = jnp.dot(
            rt[rows, :], arr[...].reshape(1024, 1024), preferred_element_type=F32
        ).astype(BF16)
        res = jnp.dot(inner, lt[...], preferred_element_type=F32).astype(BF16)
        outb[pl.ds(tx * 8, 8)] = res.reshape(8, 32, 1024)
        for j in range(8):
            k = g * 8 + j

            @pl.when(k > 0)
            def _():
                back(k)[1].start()

    ret[me] = outb[me]

    @pl.loop(0, 8)
    def _(i):
        at = pl.ds(pl.multiple_of(i * 128, 128), 128)
        tb[at, :] = jnp.transpose(arr[:, :, at].reshape(1024, 128))

    @pl.loop(0, 4)
    def _(i):
        rows = pl.ds(pl.multiple_of(i * 256, 256), 256)
        for side in (0, 1):
            if side == 0:
                gram = jnp.dot(tb[rows, :], arr[...].reshape(1024, 1024), preferred_element_type=F32)
            else:
                gram = jnp.dot(arr[pl.ds(i * 8, 8)].reshape(256, 1024), tb[...], preferred_element_type=F32)
            stat_in(i, side).wait()
            old = st[side]
            new = jnp.where(mine == 1, 0.9 * old + 0.1 * gram, old)

            @pl.when(i > 0)
            def _():
                stat_out(i - 1, side).wait()

            so[side] = new
            stat_out(i, side).start()

            @pl.when(i < 3)
            def _():
                stat_in(i + 1, side).start()

    @pl.loop(1, 32)
    def _(k):
        back(k)[1].wait()

    for r in range(14):
        update[0, :, r * 1024 : (r + 1) * 1024] = ret[owner_of[r]]
    for side in (0, 1):
        stat_out(3, side).wait()


def step(emb, hid, eg, hg, cot, own, lstat, rstat, lroot, rroot):
    dma = pltpu.SemaphoreType.DMA
    vmem = pl.BlockSpec(memory_space=pltpu.VMEM)
    hbm = pl.BlockSpec(memory_space=pl.ANY)
    return pl.pallas_call(
        reduce_kernel,
        out_shape=(
            jax.ShapeDtypeStruct((1024, 1024), F32),
            jax.ShapeDtypeStruct((1024, 1024), F32),
            jax.ShapeDtypeStruct((1, 32, 2 * WIDTH), BF16),
        ),
        in_specs=[vmem] * 5 + [pl.BlockSpec(memory_space=pltpu.SMEM)] + [hbm] * 4,
        out_specs=(hbm, hbm, vmem),
        scratch_shapes=[
            pltpu.VMEM((4, 2, 4, 4, 64, 256), BF16),
            pltpu.VMEM((2, 256, PART), BF16),
            pltpu.VMEM((4, 8, 256), F32),
            pltpu.VMEM((2, 8, 256), F32),
            pltpu.VMEM((2, 4, 4, 4, 64, HALF), BF16),
            pltpu.VMEM((2, 4, 6, 2, 64, HALF), BF16),
            pltpu.VMEM((2, 4, 6, 32, HALF), BF16),
            pltpu.VMEM((4, 2, 32, PART), BF16),
            pltpu.VMEM((8, 32, PART), BF16),
            pltpu.VMEM((14, 32, 1024), BF16),
            pltpu.VMEM((32, 32, 1024), BF16),
            pltpu.VMEM((32, 32, 1024), BF16),
            pltpu.VMEM((32, 32, 1024), BF16),
            pltpu.VMEM((1024, 1024), BF16),
            pltpu.VMEM((1024, 1024), BF16),
            pltpu.VMEM((1024, 1024), BF16),
            pltpu.VMEM((2, 256, 1024), F32),
            pltpu.VMEM((2, 256, 1024), F32),
            dma((3,)), dma((3,)), dma((2,)), dma((2,)), dma((3,)), dma((3,)), dma((4,)), dma((4,)),
            dma((2, 4, 6)), dma((2, 4, 6)), dma((2, 4, 6)), dma((2, 4, 6)), dma((4, 2)), dma((4, 2)), dma((4,)),
            dma((32,)), dma((32,)), dma((32,)), dma((32,)), dma((2,)), dma((2,)),
        ],
        compiler_params=pltpu.CompilerParams(
            collective_id=0, has_side_effects=True, vmem_limit_bytes=62 * 2**20
        ),
        name="shampoo",
    )(emb, hid, eg, hg, cot, own, lstat, rstat, lroot, rroot)


def body(
    embedding,
    hidden,
    embed_gain,
    hidden_gain,
    cotangent,
    left_stat,
    right_stat,
    left_root,
    right_root,
    owners,
):
    return step(
        embedding, hidden, embed_gain[None], hidden_gain[None], cotangent, owners,
        left_stat, right_stat, left_root, right_root,
    )


def solution(mesh):
    placed = (
        P("dp", "mp"),
        P("dp", "mp"),
        P("mp"),
        P("mp"),
        P("dp", "mp"),
        P("dp", "mp"),
        P("dp", "mp"),
        P("dp", "mp"),
        P("dp", "mp"),
        P(),
    )
    return jax.shard_map(
        body,
        mesh=mesh,
        in_specs=placed,
        out_specs=(P("dp", "mp"), P("dp", "mp"), P("mp", "dp", None)),
        check_vma=False,
    )
```

```python
import functools

import jax
import jax.numpy as jnp
from jax import lax
from jax.experimental import pallas as pl
from jax.experimental.pallas import tpu as pltpu
from jax.sharding import PartitionSpec as P

MESH = pl.DeviceIdType.MESH
F32 = jnp.float32
BF16 = jnp.bfloat16
WIDTH = 7168
PART = 1792
HALF = 896
DELTAS = (0, 1, 3, 2)


def coords():
    dp = lax.axis_index("dp")
    return dp // 8, lax.axis_index("mp"), (dp // 2) % 4, dp % 2


def device(x, y, z, core):
    return ((x * 4 + z) * 2 + core, y)


def remote(src, dst, send, recv, dest):
    return pltpu.make_async_remote_copy(
        src_ref=src, dst_ref=dst, send_sem=send, recv_sem=recv, device_id=dest, device_id_type=MESH
    )


def row_squares(ref):
    acc = jnp.zeros((256, 128), F32)
    for i in range(PART // 128):
        v = ref[:, i * 128 : (i + 1) * 128].astype(F32)
        acc = acc + v * v
    return jnp.sum(jnp.transpose(acc), axis=0, keepdims=True)


def reduce_kernel(
    emb, hid, eg, hg, cot, own, lstat, rstat, lroot, rroot, lnew, rnew, update,
    ct, nb, sq, sc, part, r1, r2, yb, sh, blocks, outb, arr, ret, tb, rt, lt, st, so,
    sq_s, sq_r, sib_s, sib_r, ct_s, ct_r, rel_s, rel_r, p1_s, p1_r, p2_s, p2_r, y_s, y_r, loc,
    o_s, o_r, b_s, b_r, st_i, st_o,
):
    x, y, z, core = coords()
    sib = device(x, y, z, 1 - core)
    nbr = {
        "x": (device((x + 1) % 4, y, z, core), device((x + 3) % 4, y, z, core), x),
        "z": (device(x, y, (z + 1) % 4, core), device(x, y, (z + 3) % 4, core), z),
    }
    barrier = pltpu.get_barrier_semaphore()
    me = (x * 4 + z) * 2 + core

    def peer_of(k):
        tx, tz, tc = (x + k // 8) % 4, (z + (k // 2) % 4) % 4, (core + k % 2) % 2
        return (tx * 4 + tz) * 2 + tc

    for d in (1, 2, 3):
        for c in (core, 1 - core):
            pl.semaphore_signal(barrier, inc=1, device_id=device(x, (y + d) % 4, z, c), device_id_type=MESH)

    for peer in (sib, *nbr["x"][:2], *nbr["z"][:2]):
        pl.semaphore_signal(barrier, inc=1, device_id=peer, device_id_type=MESH)

    r_cp = pltpu.make_async_copy(rroot, tb, loc.at[2])
    r_cp.start()

    ct[0, core] = jnp.transpose(cot[...]).reshape(4, 4, 64, 256)
    sq[core, 0] = jnp.concatenate([row_squares(emb), row_squares(hid), jnp.zeros((6, 256), F32)], axis=0)
    pl.semaphore_wait(barrier, 11)

    sends = []

    def go(cp):
        cp.start()
        sends.append(cp)
        return cp

    sq_cp = [
        go(remote(sq.at[core, 0], sq.at[core, i], sq_s.at[rel, i], sq_r.at[rel, i],
                  device(x, (y + i) % 4, z, (core + rel) % 2)))
        for i in range(4) for rel in (0, 1) if (i, rel) != (0, 0)
    ]
    ct_cp = {}
    rel_cp = {}
    rel_cp[0] = go(remote(ct.at[0, core], ct.at[0, core], rel_s.at[0], rel_r.at[0], sib))

    def along_y(s):
        ct_cp[s] = go(
            remote(ct.at[0, core], ct.at[s, core], ct_s.at[s - 1], ct_r.at[s - 1],
                   device(x, (y + 4 - DELTAS[s]) % 4, z, core))
        )

    along_y(1)
    along_y(2)
    n_cp = remote(emb, nb.at[core], sib_s.at[0], sib_r.at[0], sib)
    l_cp = pltpu.make_async_copy(emb, nb.at[core], loc.at[0])

    @pl.when(core == 0)
    def _():
        remote(hid, nb.at[core], sib_s.at[0], sib_r.at[0], sib).start()
        pltpu.make_async_copy(emb, nb.at[core], loc.at[0]).start()

    @pl.when(core == 1)
    def _():
        remote(emb, nb.at[core], sib_s.at[0], sib_r.at[0], sib).start()
        pltpu.make_async_copy(hid, nb.at[core], loc.at[0]).start()

    sends.append(n_cp)
    gain = jnp.where(core == 0, eg[...], hg[...]).reshape(1, PART)
    for cp in sq_cp:
        cp.wait_recv()
    sc[...] = lax.rsqrt((sq[:, 0] + sq[:, 1] + sq[:, 2] + sq[:, 3]) / WIDTH + 1e-6)
    l_cp.wait()
    n_cp.wait_recv()
    rel_cp[0].wait_recv()
    scale = [jnp.where(core == 0, sc[t, 0:1], sc[t, 1:2]) for t in (0, 1)]

    def relay(s):
        ct_cp[s].wait_recv()
        rel_cp[s] = go(remote(ct.at[s, core], ct.at[s, core], rel_s.at[s], rel_r.at[s], sib))

    axes = (("x", "z"), ("z", "x"))
    cps = {}

    def ring1(ab, s, u, which=range(6)):
        plus, minus, pos = nbr[axes[ab][0]]
        p1, m1, m2 = (pos + 1) % 4, (pos + 3) % 4, (pos + 2) % 4
        src = part.at[ab, u, s]

        def cp(i, ref, dest):
            return remote(ref, r1.at[ab, u, s, i], p1_s.at[ab, u, s, i], p1_r.at[ab, u, s, i], dest)

        parts = (
            (m2, slice(0, 2), plus), (m2, slice(2, 4), minus),
            (p1, slice(2, 4), plus), (m1, slice(0, 2), minus),
            (p1, slice(0, 2), plus), (m1, slice(2, 4), minus),
        )
        return [cp(w, src.at[parts[w][0], parts[w][1]], parts[w][2]) for w in which], (pos, p1, m1)

    def ring2(ab, s, u):
        plus, minus, pos = nbr[axes[ab][1]]
        p1, m1, m2 = (pos + 1) % 4, (pos + 3) % 4, (pos + 2) % 4
        src = part.at[ab, u, s, nbr[axes[ab][0]][2]]

        def cp(i, ref, dest):
            return remote(ref, r2.at[ab, u, s, i], p2_s.at[ab, u, s, i], p2_r.at[ab, u, s, i], dest)

        return [
            cp(0, src.at[m2, 0:16], plus),
            cp(1, src.at[m2, 16:32], minus),
            cp(2, src.at[p1, 16:32], plus),
            cp(3, src.at[m1, 0:16], minus),
            cp(4, src.at[p1, 0:16], plus),
            cp(5, src.at[m1, 16:32], minus),
        ], (pos, p1, m1)

    def product(s):
        if s > 0:
            rel_cp[s].wait_recv()

        @pl.loop(0, 4)
        def _(i):
            g = lax.rem(6 - i, 4)
            xg = lax.rem(x + g, 4)
            zg = lax.rem(z + g, 4)

            def lhs(t, ab):
                v = ct[s, t, xg] if ab == 0 else ct[s, t, :, zg]
                return (v.reshape(256, 256).astype(F32) * scale[t]).astype(BF16)

            for ab, at in ((0, xg), (1, zg)):
                lanes = slice(ab * HALF, (ab + 1) * HALF)
                acc = jnp.dot(lhs(0, ab), nb[0, :, lanes], preferred_element_type=F32)
                acc = acc + jnp.dot(lhs(1, ab), nb[1, :, lanes], preferred_element_type=F32)
                res = acc.astype(BF16).reshape(4, 2, 2, 16, HALF)
                for u in (0, 1):
                    part[ab, u, s, at] = res[:, :, u].reshape(4, 32, HALF)

            for turn, which in ((0, (0, 1)), (1, (2,)), (3, (3,))):

                @pl.when(i == turn)
                def _():
                    for ab in (0, 1):
                        for c in ring1(ab, s, 0, which)[0]:
                            c.start()

    def add(a, *rest):
        out = a.astype(F32)
        for r in rest:
            out = out + r.astype(F32)
        return out

    def stage_a(s, u):
        if u == 0:
            product(s)
        for ab in (0, 1):
            cps[1, ab, s, u] = ring1(ab, s, u)
            for i in range(4):
                if u == 0:
                    sends.append(cps[1, ab, s, u][0][i])
                else:
                    go(cps[1, ab, s, u][0][i])

    def stage_b(s, u):
        for ab in (0, 1):
            c, (pos, p1, m1) = cps[1, ab, s, u]
            c[0].wait_recv()
            part[ab, u, s, p1, 0:2] = add(part[ab, u, s, p1, 0:2], r1[ab, u, s, 0]).astype(BF16)
            go(c[4])
            c[1].wait_recv()
            part[ab, u, s, m1, 2:4] = add(part[ab, u, s, m1, 2:4], r1[ab, u, s, 1]).astype(BF16)
            go(c[5])

    def stage_c(s, u):
        for ab in (0, 1):
            c, (pos, p1, m1) = cps[1, ab, s, u]
            for i in (2, 3, 4, 5):
                c[i].wait_recv()
            part[ab, u, s, pos, 0:2] = add(
                part[ab, u, s, pos, 0:2], r1[ab, u, s, 4], r1[ab, u, s, 3]
            ).astype(BF16)
            part[ab, u, s, pos, 2:4] = add(
                part[ab, u, s, pos, 2:4], r1[ab, u, s, 2], r1[ab, u, s, 5]
            ).astype(BF16)
            cps[2, ab, s, u] = ring2(ab, s, u)
            for i in range(4):
                go(cps[2, ab, s, u][0][i])

    def stage_d(s, u):
        for ab in (0, 1):
            c, (pos, p1, m1) = cps[2, ab, s, u]
            o = nbr[axes[ab][0]][2]
            c[0].wait_recv()
            part[ab, u, s, o, p1, 0:16] = add(part[ab, u, s, o, p1, 0:16], r2[ab, u, s, 0]).astype(BF16)
            go(c[4])
            c[1].wait_recv()
            part[ab, u, s, o, m1, 16:32] = add(part[ab, u, s, o, m1, 16:32], r2[ab, u, s, 1]).astype(BF16)
            go(c[5])

    y_cp = {}

    def stage_e(s, u):
        for ab in (0, 1):
            c, (pos, p1, m1) = cps[2, ab, s, u]
            o = nbr[axes[ab][0]][2]
            for i in (2, 3, 4, 5):
                c[i].wait_recv()
            lanes = slice(ab * HALF, (ab + 1) * HALF)
            g = gain[:, lanes]
            for to, more in ((0, (4, 3)), (1, (2, 5))):
                yb[u, s, to, :, lanes] = (
                    add(part[ab, u, s, o, pos, 16 * to : 16 * to + 16], *[r2[ab, u, s, m] for m in more]) * g
                ).astype(BF16)
        for rel in (0, 1):
            to = (core + rel) % 2
            if s == 0 and rel == 0:
                cp = pltpu.make_async_copy(yb.at[u, s, to], sh.at[u, core * 4 + y], loc.at[u])
                cp.start()
            else:
                cp = go(
                    remote(yb.at[u, s, to], sh.at[u, core * 4 + y], y_s.at[u, s, rel], y_r.at[u, s, rel],
                           device(x, (y + DELTAS[s]) % 4, z, to))
                )
            y_cp[u, s, rel] = cp

    def transpose_root(out):
        @pl.loop(0, 8)
        def _(i):
            at = pl.ds(pl.multiple_of(i * 128, 128), 128)
            out[at, :] = jnp.transpose(tb[:, at])

    def stat_in(i, side):
        rows = pl.ds(pl.multiple_of(i * 128, 128), 128)
        return pltpu.make_async_copy((lstat, rstat)[side].at[rows], st.at[side], st_i.at[side])

    def stat_out(i, side):
        rows = pl.ds(pl.multiple_of(i * 128, 128), 128)
        return pltpu.make_async_copy(so.at[side], (lnew, rnew)[side].at[rows], st_o.at[side])

    owner_of = [own[y, r] for r in range(14)]

    def row_of(d):
        row = jnp.int32(0)
        for r in range(14):
            row = jnp.where(owner_of[r] == d, jnp.int32(r), row)
        return row

    def to_owner(k, u):
        t = peer_of(k)
        return t, remote(outb.at[t, u], arr.at[me, u], o_s.at[u, k], o_r.at[u, k], (t, y))

    def back(k):
        t = peer_of(k)
        return t, remote(outb.at[t], ret.at[me], b_s.at[k], b_r.at[k], (t, y))

    def send_owners(u):
        for s in range(4):
            for rel in (0, 1):
                if s == 0 and rel == 0:
                    y_cp[u, s, rel].wait()
                else:
                    y_cp[u, s, rel].wait_recv()
        for r in range(14):
            at = r * 1024
            done = 0
            while done < 1024:
                i, lane = (at + done) // PART, (at + done) % PART
                size = min(1024 - done, PART - lane)
                blocks[u, r, :, done : done + size] = sh[u, i, :, lane : lane + size]
                done += size

        @pl.loop(1, 32)
        def _(k):
            t, cp = to_owner(k, u)
            outb[t, u] = blocks[u, row_of(t)]
            cp.start()

        arr[me, u] = blocks[u, row_of(me)]

    chunks = ((0, 0), (0, 1), (1, 0), (2, 0), (3, 0), (1, 1), (2, 1), (3, 1))
    for turn in range(12):
        for behind, stage in enumerate((stage_a, stage_b, stage_c, stage_d, stage_e)):
            if 0 <= turn - behind < 8:
                stage(*chunks[turn - behind])
        if 1 <= turn <= 3:
            relay(turn)
        if turn == 1:
            along_y(3)
        if turn == 4:
            r_cp.wait()
            transpose_root(rt)
            l_root = pltpu.make_async_copy(lroot, tb, loc.at[3])
            l_root.start()
        if turn == 5:
            l_root.wait()
            transpose_root(lt)
            stat_in(0, 0).start()
            stat_in(0, 1).start()
        if turn == 8:
            send_owners(0)
    send_owners(1)
    mine = jnp.int32(0)
    for r in range(14):
        mine = jnp.where(owner_of[r] == me, jnp.int32(1), mine)
    for cp in sends:
        cp.wait_send()

    @pl.loop(1, 32)
    def _(k):
        for u in (0, 1):
            to_owner(k, u)[1].wait()

    @pl.loop(0, 4)
    def _(i):
        g = lax.rem(i + 1, 4)
        tx = lax.rem(x + g, 4)
        rows = pl.ds(pl.multiple_of(tx * 256, 256), 256)
        inner = jnp.dot(
            rt[rows, :], arr[...].reshape(1024, 1024), preferred_element_type=F32
        ).astype(BF16)
        res = jnp.dot(inner, lt[...], preferred_element_type=F32).astype(BF16)
        outb[pl.ds(tx * 8, 8)] = res.reshape(8, 2, 16, 1024)
        for j in range(8):
            k = g * 8 + j

            @pl.when(k > 0)
            def _():
                back(k)[1].start()

    ret[me] = outb[me]

    @pl.loop(0, 8)
    def _(i):
        at = pl.ds(pl.multiple_of(i * 128, 128), 128)
        tb[at, :] = jnp.transpose(arr[:, :, :, at].reshape(1024, 128))

    @pl.loop(0, 8)
    def _(i):
        rows = pl.ds(pl.multiple_of(i * 128, 128), 128)
        for side in (0, 1):
            if side == 0:
                gram = jnp.dot(tb[rows, :], arr[...].reshape(1024, 1024), preferred_element_type=F32)
            else:
                gram = jnp.dot(arr[pl.ds(i * 4, 4)].reshape(128, 1024), tb[...], preferred_element_type=F32)
            stat_in(i, side).wait()
            old = st[side]
            new = jnp.where(mine == 1, 0.9 * old + 0.1 * gram, old)

            @pl.when(i > 0)
            def _():
                stat_out(i - 1, side).wait()

            so[side] = new
            stat_out(i, side).start()

            @pl.when(i < 7)
            def _():
                stat_in(i + 1, side).start()

    @pl.loop(1, 32)
    def _(k):
        back(k)[1].wait()

    for r in range(14):
        update[0, :, r * 1024 : (r + 1) * 1024] = ret[owner_of[r]].reshape(32, 1024)
    for side in (0, 1):
        stat_out(7, side).wait()


def step(emb, hid, eg, hg, cot, own, lstat, rstat, lroot, rroot):
    dma = pltpu.SemaphoreType.DMA
    vmem = pl.BlockSpec(memory_space=pltpu.VMEM)
    hbm = pl.BlockSpec(memory_space=pl.ANY)
    return pl.pallas_call(
        reduce_kernel,
        out_shape=(
            jax.ShapeDtypeStruct((1024, 1024), F32),
            jax.ShapeDtypeStruct((1024, 1024), F32),
            jax.ShapeDtypeStruct((1, 32, 2 * WIDTH), BF16),
        ),
        in_specs=[vmem] * 5 + [pl.BlockSpec(memory_space=pltpu.SMEM)] + [hbm] * 4,
        out_specs=(hbm, hbm, vmem),
        scratch_shapes=[
            pltpu.VMEM((4, 2, 4, 4, 64, 256), BF16),
            pltpu.VMEM((2, 256, PART), BF16),
            pltpu.VMEM((2, 4, 8, 256), F32),
            pltpu.VMEM((2, 8, 256), F32),
            pltpu.VMEM((2, 2, 4, 4, 4, 32, HALF), BF16),
            pltpu.VMEM((2, 2, 4, 6, 2, 32, HALF), BF16),
            pltpu.VMEM((2, 2, 4, 6, 16, HALF), BF16),
            pltpu.VMEM((2, 4, 2, 16, PART), BF16),
            pltpu.VMEM((2, 8, 16, PART), BF16),
            pltpu.VMEM((2, 14, 16, 1024), BF16),
            pltpu.VMEM((32, 2, 16, 1024), BF16),
            pltpu.VMEM((32, 2, 16, 1024), BF16),
            pltpu.VMEM((32, 2, 16, 1024), BF16),
            pltpu.VMEM((1024, 1024), BF16),
            pltpu.VMEM((1024, 1024), BF16),
            pltpu.VMEM((1024, 1024), BF16),
            pltpu.VMEM((2, 128, 1024), F32),
            pltpu.VMEM((2, 128, 1024), F32),
            dma((2, 4)), dma((2, 4)), dma((1,)), dma((1,)), dma((3,)), dma((3,)), dma((4,)), dma((4,)),
            dma((2, 2, 4, 6)), dma((2, 2, 4, 6)), dma((2, 2, 4, 6)), dma((2, 2, 4, 6)),
            dma((2, 4, 2)), dma((2, 4, 2)), dma((4,)),
            dma((2, 32)), dma((2, 32)), dma((32,)), dma((32,)), dma((2,)), dma((2,)),
        ],
        compiler_params=pltpu.CompilerParams(
            collective_id=0, has_side_effects=True, vmem_limit_bytes=62 * 2**20
        ),
        name="shampoo",
    )(emb, hid, eg, hg, cot, own, lstat, rstat, lroot, rroot)


def body(
    embedding,
    hidden,
    embed_gain,
    hidden_gain,
    cotangent,
    left_stat,
    right_stat,
    left_root,
    right_root,
    owners,
):
    return step(
        embedding, hidden, embed_gain, hidden_gain, cotangent, owners,
        left_stat, right_stat, left_root, right_root,
    )


def solution(mesh):
    placed = (
        P("dp", "mp"),
        P("dp", "mp"),
        P("mp"),
        P("mp"),
        P("dp", "mp"),
        P("dp", "mp"),
        P("dp", "mp"),
        P("dp", "mp"),
        P("dp", "mp"),
        P(),
    )
    return jax.shard_map(
        body,
        mesh=mesh,
        in_specs=placed,
        out_specs=(P("dp", "mp"), P("dp", "mp"), P("mp", "dp", None)),
        check_vma=False,
    )
```

```python
import functools

import jax
import jax.numpy as jnp
from jax import lax
from jax.experimental import pallas as pl
from jax.experimental.pallas import tpu as pltpu
from jax.sharding import PartitionSpec as P

MESH = pl.DeviceIdType.MESH
F32 = jnp.float32
BF16 = jnp.bfloat16
WIDTH = 7168
PART = 1792
HALF = 896
DELTAS = (0, 1, 3, 2)


def coords():
    dp = lax.axis_index("dp")
    return dp // 8, lax.axis_index("mp"), (dp // 2) % 4, dp % 2


def device(x, y, z, core):
    return ((x * 4 + z) * 2 + core, y)


def remote(src, dst, send, recv, dest):
    return pltpu.make_async_remote_copy(
        src_ref=src, dst_ref=dst, send_sem=send, recv_sem=recv, device_id=dest, device_id_type=MESH
    )


def row_squares(ref):
    acc = jnp.zeros((256, 128), F32)
    for i in range(PART // 128):
        v = ref[:, i * 128 : (i + 1) * 128].astype(F32)
        acc = acc + v * v
    return jnp.sum(jnp.transpose(acc), axis=0, keepdims=True)


def reduce_kernel(
    emb, hid, eg, hg, cot, own, lstat, rstat, lroot, rroot, lnew, rnew, update,
    ct, nb, sq, sc, part, r1, r2, yb, sh, blocks, outb, arr, ret, tb, rt, lt, st, so, mid, midb,
    sq_s, sq_r, sib_s, sib_r, ct_s, ct_r, rel_s, rel_r, p1_s, p1_r, p2_s, p2_r, y_s, y_r, loc,
    o_s, o_r, q_s, q_r, b_s, b_r, c_s, c_r, st_i, st_o,
):
    x, y, z, core = coords()
    sib = device(x, y, z, 1 - core)
    nbr = {
        "x": (device((x + 1) % 4, y, z, core), device((x + 3) % 4, y, z, core), x),
        "z": (device(x, y, (z + 1) % 4, core), device(x, y, (z + 3) % 4, core), z),
    }
    barrier = pltpu.get_barrier_semaphore()
    me = (x * 4 + z) * 2 + core

    for d in (1, 2, 3):
        for c in (core, 1 - core):
            pl.semaphore_signal(barrier, inc=1, device_id=device(x, (y + d) % 4, z, c), device_id_type=MESH)

    for peer in (sib, *nbr["x"][:2], *nbr["z"][:2]):
        pl.semaphore_signal(barrier, inc=1, device_id=peer, device_id_type=MESH)

    r_cp = pltpu.make_async_copy(rroot, tb, loc.at[2])
    r_cp.start()

    ct[0, core] = jnp.transpose(cot[...]).reshape(4, 4, 64, 256)
    sq[core, 0] = jnp.concatenate([row_squares(emb), row_squares(hid), jnp.zeros((6, 256), F32)], axis=0)
    pl.semaphore_wait(barrier, 11)

    sends = []

    def go(cp):
        cp.start()
        sends.append(cp)
        return cp

    sq_cp = [
        go(remote(sq.at[core, 0], sq.at[core, i], sq_s.at[rel, i], sq_r.at[rel, i],
                  device(x, (y + i) % 4, z, (core + rel) % 2)))
        for i in range(4) for rel in (0, 1) if (i, rel) != (0, 0)
    ]
    ct_cp = {}
    rel_cp = {}
    rel_cp[0] = go(remote(ct.at[0, core], ct.at[0, core], rel_s.at[0], rel_r.at[0], sib))

    def along_y(s):
        ct_cp[s] = go(
            remote(ct.at[0, core], ct.at[s, core], ct_s.at[s - 1], ct_r.at[s - 1],
                   device(x, (y + 4 - DELTAS[s]) % 4, z, core))
        )

    along_y(1)
    along_y(2)
    n_cp = remote(emb, nb.at[core], sib_s.at[0], sib_r.at[0], sib)
    l_cp = pltpu.make_async_copy(emb, nb.at[core], loc.at[0])

    @pl.when(core == 0)
    def _():
        remote(hid, nb.at[core], sib_s.at[0], sib_r.at[0], sib).start()
        pltpu.make_async_copy(emb, nb.at[core], loc.at[0]).start()

    @pl.when(core == 1)
    def _():
        remote(emb, nb.at[core], sib_s.at[0], sib_r.at[0], sib).start()
        pltpu.make_async_copy(hid, nb.at[core], loc.at[0]).start()

    sends.append(n_cp)
    gain = jnp.where(core == 0, eg[...], hg[...]).reshape(1, PART)
    for cp in sq_cp:
        cp.wait_recv()
    sc[...] = lax.rsqrt((sq[:, 0] + sq[:, 1] + sq[:, 2] + sq[:, 3]) / WIDTH + 1e-6)
    l_cp.wait()
    n_cp.wait_recv()
    rel_cp[0].wait_recv()
    scale = [jnp.where(core == 0, sc[t, 0:1], sc[t, 1:2]) for t in (0, 1)]

    def relay(s):
        ct_cp[s].wait_recv()
        rel_cp[s] = go(remote(ct.at[s, core], ct.at[s, core], rel_s.at[s], rel_r.at[s], sib))

    axes = (("x", "z"), ("z", "x"))
    cps = {}

    def ring1(ab, s, u, which=range(6)):
        plus, minus, pos = nbr[axes[ab][0]]
        p1, m1, m2 = (pos + 1) % 4, (pos + 3) % 4, (pos + 2) % 4
        src = part.at[ab, u, s]

        def cp(i, ref, dest):
            return remote(ref, r1.at[ab, u, s, i], p1_s.at[ab, u, s, i], p1_r.at[ab, u, s, i], dest)

        parts = (
            (m2, slice(0, 2), plus), (m2, slice(2, 4), minus),
            (p1, slice(2, 4), plus), (m1, slice(0, 2), minus),
            (p1, slice(0, 2), plus), (m1, slice(2, 4), minus),
        )
        return [cp(w, src.at[parts[w][0], parts[w][1]], parts[w][2]) for w in which], (pos, p1, m1)

    def ring2(ab, s, u):
        plus, minus, pos = nbr[axes[ab][1]]
        p1, m1, m2 = (pos + 1) % 4, (pos + 3) % 4, (pos + 2) % 4
        src = part.at[ab, u, s, nbr[axes[ab][0]][2]]

        def cp(i, ref, dest):
            return remote(ref, r2.at[ab, u, s, i], p2_s.at[ab, u, s, i], p2_r.at[ab, u, s, i], dest)

        return [
            cp(0, src.at[m2, 0:16], plus),
            cp(1, src.at[m2, 16:32], minus),
            cp(2, src.at[p1, 16:32], plus),
            cp(3, src.at[m1, 0:16], minus),
            cp(4, src.at[p1, 0:16], plus),
            cp(5, src.at[m1, 16:32], minus),
        ], (pos, p1, m1)

    def product(s):
        if s > 0:
            rel_cp[s].wait_recv()

        @pl.loop(0, 4)
        def _(i):
            g = lax.rem(6 - i, 4)
            xg = lax.rem(x + g, 4)
            zg = lax.rem(z + g, 4)

            def lhs(t, ab):
                v = ct[s, t, xg] if ab == 0 else ct[s, t, :, zg]
                return (v.reshape(256, 256).astype(F32) * scale[t]).astype(BF16)

            for ab, at in ((0, xg), (1, zg)):
                lanes = slice(ab * HALF, (ab + 1) * HALF)
                acc = jnp.dot(lhs(0, ab), nb[0, :, lanes], preferred_element_type=F32)
                acc = acc + jnp.dot(lhs(1, ab), nb[1, :, lanes], preferred_element_type=F32)
                res = acc.astype(BF16).reshape(4, 2, 2, 16, HALF)
                for u in (0, 1):
                    part[ab, u, s, at] = res[:, :, u].reshape(4, 32, HALF)

            for turn, which in ((0, (0, 1)), (1, (2,)), (3, (3,))):

                @pl.when(i == turn)
                def _():
                    for ab in (0, 1):
                        for c in ring1(ab, s, 0, which)[0]:
                            c.start()

    def add(a, *rest):
        out = a.astype(F32)
        for r in rest:
            out = out + r.astype(F32)
        return out

    def stage_a(s, u):
        if u == 0:
            product(s)
        for ab in (0, 1):
            cps[1, ab, s, u] = ring1(ab, s, u)
            for i in range(4):
                if u == 0:
                    sends.append(cps[1, ab, s, u][0][i])
                else:
                    go(cps[1, ab, s, u][0][i])

    def stage_b(s, u):
        for ab in (0, 1):
            c, (pos, p1, m1) = cps[1, ab, s, u]
            c[0].wait_recv()
            part[ab, u, s, p1, 0:2] = add(part[ab, u, s, p1, 0:2], r1[ab, u, s, 0]).astype(BF16)
            go(c[4])
            c[1].wait_recv()
            part[ab, u, s, m1, 2:4] = add(part[ab, u, s, m1, 2:4], r1[ab, u, s, 1]).astype(BF16)
            go(c[5])

    def stage_c(s, u):
        for ab in (0, 1):
            c, (pos, p1, m1) = cps[1, ab, s, u]
            for i in (2, 3, 4, 5):
                c[i].wait_recv()
            part[ab, u, s, pos, 0:2] = add(
                part[ab, u, s, pos, 0:2], r1[ab, u, s, 4], r1[ab, u, s, 3]
            ).astype(BF16)
            part[ab, u, s, pos, 2:4] = add(
                part[ab, u, s, pos, 2:4], r1[ab, u, s, 2], r1[ab, u, s, 5]
            ).astype(BF16)
            cps[2, ab, s, u] = ring2(ab, s, u)
            for i in range(4):
                go(cps[2, ab, s, u][0][i])

    def stage_d(s, u):
        for ab in (0, 1):
            c, (pos, p1, m1) = cps[2, ab, s, u]
            o = nbr[axes[ab][0]][2]
            c[0].wait_recv()
            part[ab, u, s, o, p1, 0:16] = add(part[ab, u, s, o, p1, 0:16], r2[ab, u, s, 0]).astype(BF16)
            go(c[4])
            c[1].wait_recv()
            part[ab, u, s, o, m1, 16:32] = add(part[ab, u, s, o, m1, 16:32], r2[ab, u, s, 1]).astype(BF16)
            go(c[5])

    y_cp = {}

    def stage_e(s, u):
        for ab in (0, 1):
            c, (pos, p1, m1) = cps[2, ab, s, u]
            o = nbr[axes[ab][0]][2]
            for i in (2, 3, 4, 5):
                c[i].wait_recv()
            lanes = slice(ab * HALF, (ab + 1) * HALF)
            g = gain[:, lanes]
            for to, more in ((0, (4, 3)), (1, (2, 5))):
                yb[u, s, to, :, lanes] = (
                    add(part[ab, u, s, o, pos, 16 * to : 16 * to + 16], *[r2[ab, u, s, m] for m in more]) * g
                ).astype(BF16)
        for rel in (0, 1):
            to = (core + rel) % 2
            if s == 0 and rel == 0:
                cp = pltpu.make_async_copy(yb.at[u, s, to], sh.at[u, core * 4 + y], loc.at[u])
                cp.start()
            else:
                cp = go(
                    remote(yb.at[u, s, to], sh.at[u, core * 4 + y], y_s.at[u, s, rel], y_r.at[u, s, rel],
                           device(x, (y + DELTAS[s]) % 4, z, to))
                )
            y_cp[u, s, rel] = cp

    def transpose_root(out):
        @pl.loop(0, 8)
        def _(i):
            at = pl.ds(pl.multiple_of(i * 128, 128), 128)
            out[at, :] = jnp.transpose(tb[:, at])

    def stat_in(i, side):
        rows = pl.ds(pl.multiple_of(i * 128, 128), 128)
        return pltpu.make_async_copy((lstat, rstat)[side].at[rows], st.at[side], st_i.at[side])

    def stat_out(i, side):
        rows = pl.ds(pl.multiple_of(i * 128, 128), 128)
        return pltpu.make_async_copy(so.at[side], (lnew, rnew)[side].at[rows], st_o.at[side])

    owner_of = [own[y, r] for r in range(14)]

    def row_of(d):
        row = jnp.int32(0)
        for r in range(14):
            row = jnp.where(owner_of[r] == d, jnp.int32(r), row)
        return row

    def line(ab, d):
        return ((x + d) % 4, z) if ab == 0 else (x, (z + d) % 4)

    def spread(src_of, mid, ab, d, send, recv):
        tx, tz = line(ab, d)
        here = x if ab == 0 else z
        return remote(src_of(ab, tx if ab == 0 else tz), mid.at[here], send, recv, device(tx, y, tz, core))

    def deliver(mid, dst_of, ab, d, dc, send, recv):
        tx, tz = line(1 - ab, d)
        tc = (core + dc) % 2
        return remote(mid.at[:, tz if ab == 0 else tx, tc], dst_of(ab), send, recv, device(tx, y, tz, tc))

    HOPS = [(d, dc) for d in (2, 1, 3, 0) for dc in (0, 1) if (d, dc) != (0, 0)]

    def owner_src(u):
        def src_of(ab, at):
            lanes = pl.ds(512 * ab, 512)
            return outb.at[at, :, :, u, :, lanes] if ab == 0 else outb.at[:, at, :, u, :, lanes]

        return src_of

    def owner_dst(u):
        def dst_of(ab):
            lanes = pl.ds(512 * ab, 512)
            return arr.at[:, z, core, u, :, lanes] if ab == 0 else arr.at[x, :, core, u, :, lanes]

        return dst_of

    def owner_spread(u):
        return [
            spread(owner_src(u), mid.at[u, ab], ab, d, o_s.at[u, ab, d], o_r.at[u, ab, d])
            for d in (2, 1, 3) for ab in (0, 1)
        ]

    def owner_deliver(u):
        return [
            deliver(mid.at[u, ab], owner_dst(u), ab, d, dc, q_s.at[u, ab, d, dc], q_r.at[u, ab, d, dc])
            for d, dc in HOPS for ab in (0, 1)
        ]

    def back_src(ab, at):
        return outb.at[at, :, :, 0] if ab == 0 else outb.at[:, at, :, 1]

    def back_dst(ab):
        return ret.at[:, z, core, 0] if ab == 0 else ret.at[x, :, core, 1]

    def back_spread(ab, d):
        return spread(back_src, midb.at[ab], ab, d, b_s.at[ab, d], b_r.at[ab, d])

    def back_deliver(ab, d, dc):
        return deliver(midb.at[ab], back_dst, ab, d, dc, c_s.at[ab, d, dc], c_r.at[ab, d, dc])

    passing = {}

    def send_owners(u):
        for s in range(4):
            for rel in (0, 1):
                if s == 0 and rel == 0:
                    y_cp[u, s, rel].wait()
                else:
                    y_cp[u, s, rel].wait_recv()
        for r in range(14):
            at = r * 1024
            done = 0
            while done < 1024:
                i, lane = (at + done) // PART, (at + done) % PART
                size = min(1024 - done, PART - lane)
                blocks[u, r, :, done : done + size] = sh[u, i, :, lane : lane + size]
                done += size

        @pl.loop(0, 32)
        def _(t):
            outb[t // 8, (t // 2) % 4, t % 2, u] = blocks[u, row_of(t)]

        passing[1, u] = owner_spread(u)
        for cp in passing[1, u]:
            go(cp)
        mid[u, 0, x] = outb[x, :, :, u, :, 0:512]
        mid[u, 1, z] = outb[:, z, :, u, :, 512:1024]

    def pass_owners(u):
        for cp in passing[1, u]:
            cp.wait_recv()
        passing[2, u] = owner_deliver(u)
        for cp in passing[2, u]:
            go(cp)
        arr[:, z, core, u, :, 0:512] = mid[u, 0, :, z, core]
        arr[x, :, core, u, :, 512:1024] = mid[u, 1, :, x, core]

    chunks = ((0, 0), (0, 1), (1, 0), (2, 0), (3, 0), (1, 1), (2, 1), (3, 1))
    for turn in range(12):
        for behind, stage in enumerate((stage_a, stage_b, stage_c, stage_d, stage_e)):
            if 0 <= turn - behind < 8:
                stage(*chunks[turn - behind])
        if 1 <= turn <= 3:
            relay(turn)
        if turn == 1:
            along_y(3)
        if turn == 4:
            r_cp.wait()
            transpose_root(rt)
            l_root = pltpu.make_async_copy(lroot, tb, loc.at[3])
            l_root.start()
        if turn == 5:
            l_root.wait()
            transpose_root(lt)
            stat_in(0, 0).start()
            stat_in(0, 1).start()
        if turn == 8:
            send_owners(0)
        if turn == 10:
            pass_owners(0)
    send_owners(1)
    pass_owners(1)
    mine = jnp.int32(0)
    for r in range(14):
        mine = jnp.where(owner_of[r] == me, jnp.int32(1), mine)
    for u in (0, 1):
        for cp in passing[2, u]:
            cp.wait_recv()
    for cp in sends:
        cp.wait_send()

    @pl.loop(0, 4)
    def _(i):
        g = lax.rem(6 - i, 4)
        tx = lax.rem(x + g, 4)
        rows = pl.ds(pl.multiple_of(tx * 256, 256), 256)
        inner = jnp.dot(
            rt[rows, :], arr[...].reshape(1024, 1024), preferred_element_type=F32
        ).astype(BF16)
        res = jnp.dot(inner, lt[...], preferred_element_type=F32).astype(BF16)
        outb[tx] = res.reshape(4, 2, 2, 16, 1024)
        for turn, d in ((0, 2), (1, 1), (3, 3)):

            @pl.when(i == turn)
            def _():
                back_spread(0, d).start()

    for d in (2, 1, 3):
        back_spread(1, d).start()
    midb[0, x] = outb[x, :, :, 0]
    midb[1, z] = outb[:, z, :, 1]

    @pl.loop(0, 8)
    def _(i):
        at = pl.ds(pl.multiple_of(i * 128, 128), 128)
        for w in range(4):
            tb[at, w * 256 : (w + 1) * 256] = jnp.transpose(arr[w, :, :, :, :, at].reshape(256, 128))

    def grams(first, last):
        @pl.loop(first, last)
        def _(i):
            rows = pl.ds(pl.multiple_of(i * 128, 128), 128)
            for side in (0, 1):
                if side == 0:
                    gram = jnp.dot(tb[rows, :], arr[...].reshape(1024, 1024), preferred_element_type=F32)
                else:
                    mine_rows = arr[i // 2, pl.ds(2 * (i % 2), 2)].reshape(128, 1024)
                    gram = jnp.dot(mine_rows, tb[...], preferred_element_type=F32)
                stat_in(i, side).wait()
                old = st[side]
                new = jnp.where(mine == 1, 0.9 * old + 0.1 * gram, old)

                @pl.when(i > 0)
                def _():
                    stat_out(i - 1, side).wait()

                so[side] = new
                stat_out(i, side).start()

                @pl.when(i < 7)
                def _():
                    stat_in(i + 1, side).start()

    grams(0, 4)
    for d in (2, 1, 3):
        for ab in (0, 1):
            back_spread(ab, d).wait_recv()
    last = [back_deliver(ab, d, dc) for d, dc in HOPS for ab in (0, 1)]
    for cp in last:
        cp.start()
    ret[:, z, core, 0] = midb[0, :, z, core]
    ret[x, :, core, 1] = midb[1, :, x, core]
    grams(4, 8)
    for cp in last:
        cp.wait()
    for d in (2, 1, 3):
        for ab in (0, 1):
            back_spread(ab, d).wait_send()

    for r in range(14):
        update[0, :, r * 1024 : (r + 1) * 1024] = ret[
            owner_of[r] // 8, (owner_of[r] // 2) % 4, owner_of[r] % 2
        ].reshape(32, 1024)
    for side in (0, 1):
        stat_out(7, side).wait()


def step(emb, hid, eg, hg, cot, own, lstat, rstat, lroot, rroot):
    dma = pltpu.SemaphoreType.DMA
    vmem = pl.BlockSpec(memory_space=pltpu.VMEM)
    hbm = pl.BlockSpec(memory_space=pl.ANY)
    return pl.pallas_call(
        reduce_kernel,
        out_shape=(
            jax.ShapeDtypeStruct((1024, 1024), F32),
            jax.ShapeDtypeStruct((1024, 1024), F32),
            jax.ShapeDtypeStruct((1, 32, 2 * WIDTH), BF16),
        ),
        in_specs=[vmem] * 5 + [pl.BlockSpec(memory_space=pltpu.SMEM)] + [hbm] * 4,
        out_specs=(hbm, hbm, vmem),
        scratch_shapes=[
            pltpu.VMEM((4, 2, 4, 4, 64, 256), BF16),
            pltpu.VMEM((2, 256, PART), BF16),
            pltpu.VMEM((2, 4, 8, 256), F32),
            pltpu.VMEM((2, 8, 256), F32),
            pltpu.VMEM((2, 2, 4, 4, 4, 32, HALF), BF16),
            pltpu.VMEM((2, 2, 4, 6, 2, 32, HALF), BF16),
            pltpu.VMEM((2, 2, 4, 6, 16, HALF), BF16),
            pltpu.VMEM((2, 4, 2, 16, PART), BF16),
            pltpu.VMEM((2, 8, 16, PART), BF16),
            pltpu.VMEM((2, 14, 16, 1024), BF16),
            pltpu.VMEM((4, 4, 2, 2, 16, 1024), BF16),
            pltpu.VMEM((4, 4, 2, 2, 16, 1024), BF16),
            pltpu.VMEM((4, 4, 2, 2, 16, 1024), BF16),
            pltpu.VMEM((1024, 1024), BF16),
            pltpu.VMEM((1024, 1024), BF16),
            pltpu.VMEM((1024, 1024), BF16),
            pltpu.VMEM((2, 128, 1024), F32),
            pltpu.VMEM((2, 128, 1024), F32),
            pltpu.VMEM((2, 2, 4, 4, 2, 16, 512), BF16),
            pltpu.VMEM((2, 4, 4, 2, 16, 1024), BF16),
            dma((2, 4)), dma((2, 4)), dma((1,)), dma((1,)), dma((3,)), dma((3,)), dma((4,)), dma((4,)),
            dma((2, 2, 4, 6)), dma((2, 2, 4, 6)), dma((2, 2, 4, 6)), dma((2, 2, 4, 6)),
            dma((2, 4, 2)), dma((2, 4, 2)), dma((4,)),
            dma((2, 2, 4)), dma((2, 2, 4)), dma((2, 2, 4, 2)), dma((2, 2, 4, 2)),
            dma((2, 4)), dma((2, 4)), dma((2, 4, 2)), dma((2, 4, 2)), dma((2,)), dma((2,)),
        ],
        compiler_params=pltpu.CompilerParams(
            collective_id=0, has_side_effects=True, vmem_limit_bytes=62 * 2**20
        ),
        name="shampoo",
    )(emb, hid, eg, hg, cot, own, lstat, rstat, lroot, rroot)


def body(
    embedding,
    hidden,
    embed_gain,
    hidden_gain,
    cotangent,
    left_stat,
    right_stat,
    left_root,
    right_root,
    owners,
):
    return step(
        embedding, hidden, embed_gain, hidden_gain, cotangent, owners,
        left_stat, right_stat, left_root, right_root,
    )


def solution(mesh):
    placed = (
        P("dp", "mp"),
        P("dp", "mp"),
        P("mp"),
        P("mp"),
        P("dp", "mp"),
        P("dp", "mp"),
        P("dp", "mp"),
        P("dp", "mp"),
        P("dp", "mp"),
        P(),
    )
    return jax.shard_map(
        body,
        mesh=mesh,
        in_specs=placed,
        out_specs=(P("dp", "mp"), P("dp", "mp"), P("mp", "dp", None)),
        check_vma=False,
    )
```

```python
import functools

import jax
import jax.numpy as jnp
from jax import lax
from jax.experimental import pallas as pl
from jax.experimental.pallas import tpu as pltpu
from jax.sharding import PartitionSpec as P

MESH = pl.DeviceIdType.MESH
F32 = jnp.float32
BF16 = jnp.bfloat16
WIDTH = 7168
PART = 1792
HALF = 896
DELTAS = (0, 1, 3, 2)


def coords():
    dp = lax.axis_index("dp")
    return dp // 8, lax.axis_index("mp"), (dp // 2) % 4, dp % 2


def device(x, y, z, core):
    return ((x * 4 + z) * 2 + core, y)


def remote(src, dst, send, recv, dest):
    return pltpu.make_async_remote_copy(
        src_ref=src, dst_ref=dst, send_sem=send, recv_sem=recv, device_id=dest, device_id_type=MESH
    )


def row_squares(ref):
    acc = jnp.zeros((256, 128), F32)
    for i in range(PART // 128):
        v = ref[:, i * 128 : (i + 1) * 128].astype(F32)
        acc = acc + v * v
    return jnp.sum(jnp.transpose(acc), axis=0, keepdims=True)


def reduce_kernel(
    emb, hid, eg, hg, cot, own, lstat, rstat, lroot, rroot, lnew, rnew, update,
    ct, nb, sq, sc, part, r1, r2, yb, sh, blocks, outb, arr, ret, tb, rt, lt, st, so, mid, midb,
    sq_s, sq_r, sib_s, sib_r, ct_s, ct_r, rel_s, rel_r, p1_s, p1_r, p2_s, p2_r, y_s, y_r, loc,
    o_s, o_r, q_s, q_r, b_s, b_r, c_s, c_r, t_s, t_r, st_i, st_o,
):
    x, y, z, core = coords()
    sib = device(x, y, z, 1 - core)
    nbr = {
        "x": (device((x + 1) % 4, y, z, core), device((x + 3) % 4, y, z, core), x),
        "z": (device(x, y, (z + 1) % 4, core), device(x, y, (z + 3) % 4, core), z),
    }
    barrier = pltpu.get_barrier_semaphore()
    me = (x * 4 + z) * 2 + core

    for d in (1, 2, 3):
        for c in (core, 1 - core):
            pl.semaphore_signal(barrier, inc=1, device_id=device(x, (y + d) % 4, z, c), device_id_type=MESH)

    for peer in (sib, *nbr["x"][:2], *nbr["z"][:2]):
        pl.semaphore_signal(barrier, inc=1, device_id=peer, device_id_type=MESH)

    r_cp = pltpu.make_async_copy(rroot, tb, loc.at[2])
    r_cp.start()

    ct[0, core] = jnp.transpose(cot[...]).reshape(4, 4, 64, 256)
    sq[core, 0] = jnp.concatenate([row_squares(emb), row_squares(hid), jnp.zeros((6, 256), F32)], axis=0)

    @pl.when(core == 0)
    def _():
        nb[0] = emb[...]

    @pl.when(core == 1)
    def _():
        nb[1] = hid[...]

    pl.semaphore_wait(barrier, 11)

    sends = []

    def go(cp):
        cp.start()
        sends.append(cp)
        return cp

    sq_cp = [
        go(remote(sq.at[core, 0], sq.at[core, i], sq_s.at[rel, i], sq_r.at[rel, i],
                  device(x, (y + i) % 4, z, (core + rel) % 2)))
        for i in range(4) for rel in (0, 1) if (i, rel) != (0, 0)
    ]
    ct_cp = {}
    rel_cp = {}
    rel_cp[0] = go(remote(ct.at[0, core], ct.at[0, core], rel_s.at[0], rel_r.at[0], sib))

    def along_y(s):
        ct_cp[s] = go(
            remote(ct.at[0, core], ct.at[s, core], ct_s.at[s - 1], ct_r.at[s - 1],
                   device(x, (y + 4 - DELTAS[s]) % 4, z, core))
        )

    along_y(1)
    along_y(2)
    n_cp = remote(emb, nb.at[core], sib_s.at[0], sib_r.at[0], sib)

    @pl.when(core == 0)
    def _():
        remote(hid, nb.at[core], sib_s.at[0], sib_r.at[0], sib).start()

    @pl.when(core == 1)
    def _():
        remote(emb, nb.at[core], sib_s.at[0], sib_r.at[0], sib).start()

    sends.append(n_cp)
    gain = jnp.where(core == 0, eg[...], hg[...]).reshape(1, PART)
    for cp in sq_cp:
        cp.wait_recv()
    sc[...] = lax.rsqrt((sq[:, 0] + sq[:, 1] + sq[:, 2] + sq[:, 3]) / WIDTH + 1e-6)
    n_cp.wait_recv()
    rel_cp[0].wait_recv()
    scale = [jnp.where(core == 0, sc[t, 0:1], sc[t, 1:2]) for t in (0, 1)]

    def relay(s):
        ct_cp[s].wait_recv()
        rel_cp[s] = go(remote(ct.at[s, core], ct.at[s, core], rel_s.at[s], rel_r.at[s], sib))

    axes = (("x", "z"), ("z", "x"))
    cps = {}

    def ring1(ab, s, u, which=range(6)):
        plus, minus, pos = nbr[axes[ab][0]]
        p1, m1, m2 = (pos + 1) % 4, (pos + 3) % 4, (pos + 2) % 4
        src = part.at[ab, u, s]

        def cp(i, ref, dest):
            return remote(ref, r1.at[ab, u, s, i], p1_s.at[ab, u, s, i], p1_r.at[ab, u, s, i], dest)

        parts = (
            (m2, slice(0, 2), plus), (m2, slice(2, 4), minus),
            (p1, slice(2, 4), plus), (m1, slice(0, 2), minus),
            (p1, slice(0, 2), plus), (m1, slice(2, 4), minus),
        )
        return [cp(w, src.at[parts[w][0], parts[w][1]], parts[w][2]) for w in which], (pos, p1, m1)

    def ring2(ab, s, u):
        plus, minus, pos = nbr[axes[ab][1]]
        p1, m1, m2 = (pos + 1) % 4, (pos + 3) % 4, (pos + 2) % 4
        src = part.at[ab, u, s, nbr[axes[ab][0]][2]]

        def cp(i, ref, dest):
            return remote(ref, r2.at[ab, u, s, i], p2_s.at[ab, u, s, i], p2_r.at[ab, u, s, i], dest)

        return [
            cp(0, src.at[m2, 0:16], plus),
            cp(1, src.at[m2, 16:32], minus),
            cp(2, src.at[p1, 16:32], plus),
            cp(3, src.at[m1, 0:16], minus),
            cp(4, src.at[p1, 0:16], plus),
            cp(5, src.at[m1, 16:32], minus),
        ], (pos, p1, m1)

    def product(s):
        if s > 0:
            rel_cp[s].wait_recv()

        @pl.loop(0, 4)
        def _(i):
            g = lax.rem(6 - i, 4)
            xg = lax.rem(x + g, 4)
            zg = lax.rem(z + g, 4)

            def lhs(t, ab):
                v = ct[s, t, xg] if ab == 0 else ct[s, t, :, zg]
                return (v.reshape(256, 256).astype(F32) * scale[t]).astype(BF16)

            for ab, at in ((0, xg), (1, zg)):
                lanes = slice(ab * HALF, (ab + 1) * HALF)
                acc = jnp.dot(lhs(0, ab), nb[0, :, lanes], preferred_element_type=F32)
                acc = acc + jnp.dot(lhs(1, ab), nb[1, :, lanes], preferred_element_type=F32)
                res = acc.astype(BF16).reshape(4, 2, 2, 16, HALF)
                for u in (0, 1):
                    part[ab, u, s, at] = res[:, :, u].reshape(4, 32, HALF)

            for turn, which in ((0, (0, 1)), (1, (2,)), (3, (3,))):

                @pl.when(i == turn)
                def _():
                    for ab in (0, 1):
                        for c in ring1(ab, s, 0, which)[0]:
                            c.start()

    def add(a, *rest):
        out = a.astype(F32)
        for r in rest:
            out = out + r.astype(F32)
        return out

    def stage_a(s, u):
        if u == 0:
            product(s)
        for ab in (0, 1):
            cps[1, ab, s, u] = ring1(ab, s, u)
            for i in range(4):
                if u == 0:
                    sends.append(cps[1, ab, s, u][0][i])
                else:
                    go(cps[1, ab, s, u][0][i])

    def stage_b(s, u):
        for ab in (0, 1):
            c, (pos, p1, m1) = cps[1, ab, s, u]
            c[0].wait_recv()
            part[ab, u, s, p1, 0:2] = add(part[ab, u, s, p1, 0:2], r1[ab, u, s, 0]).astype(BF16)
            go(c[4])
            c[1].wait_recv()
            part[ab, u, s, m1, 2:4] = add(part[ab, u, s, m1, 2:4], r1[ab, u, s, 1]).astype(BF16)
            go(c[5])

    def stage_c(s, u):
        for ab in (0, 1):
            c, (pos, p1, m1) = cps[1, ab, s, u]
            for i in (2, 3, 4, 5):
                c[i].wait_recv()
            part[ab, u, s, pos, 0:2] = add(
                part[ab, u, s, pos, 0:2], r1[ab, u, s, 4], r1[ab, u, s, 3]
            ).astype(BF16)
            part[ab, u, s, pos, 2:4] = add(
                part[ab, u, s, pos, 2:4], r1[ab, u, s, 2], r1[ab, u, s, 5]
            ).astype(BF16)
            cps[2, ab, s, u] = ring2(ab, s, u)
            for i in range(4):
                go(cps[2, ab, s, u][0][i])

    def stage_d(s, u):
        for ab in (0, 1):
            c, (pos, p1, m1) = cps[2, ab, s, u]
            o = nbr[axes[ab][0]][2]
            c[0].wait_recv()
            part[ab, u, s, o, p1, 0:16] = add(part[ab, u, s, o, p1, 0:16], r2[ab, u, s, 0]).astype(BF16)
            go(c[4])
            c[1].wait_recv()
            part[ab, u, s, o, m1, 16:32] = add(part[ab, u, s, o, m1, 16:32], r2[ab, u, s, 1]).astype(BF16)
            go(c[5])

    y_cp = {}

    def stage_e(s, u):
        for ab in (0, 1):
            c, (pos, p1, m1) = cps[2, ab, s, u]
            o = nbr[axes[ab][0]][2]
            for i in (2, 3, 4, 5):
                c[i].wait_recv()
            lanes = slice(ab * HALF, (ab + 1) * HALF)
            g = gain[:, lanes]
            for to, more in ((0, (4, 3)), (1, (2, 5))):
                yb[u, s, to, :, lanes] = (
                    add(part[ab, u, s, o, pos, 16 * to : 16 * to + 16], *[r2[ab, u, s, m] for m in more]) * g
                ).astype(BF16)
        for rel in (0, 1):
            to = (core + rel) % 2
            if s == 0 and rel == 0:
                cp = pltpu.make_async_copy(yb.at[u, s, to], sh.at[u, core * 4 + y], loc.at[u])
                cp.start()
            else:
                cp = go(
                    remote(yb.at[u, s, to], sh.at[u, core * 4 + y], y_s.at[u, s, rel], y_r.at[u, s, rel],
                           device(x, (y + DELTAS[s]) % 4, z, to))
                )
            y_cp[u, s, rel] = cp

    def transpose_root(out):
        @pl.loop(0, 8)
        def _(i):
            at = pl.ds(pl.multiple_of(i * 128, 128), 128)
            out[at, :] = jnp.transpose(tb[:, at])

    def stat_in(i, side):
        rows = pl.ds(pl.multiple_of(i * 128, 128), 128)
        return pltpu.make_async_copy((lstat, rstat)[side].at[rows], st.at[side], st_i.at[side])

    def stat_out(i, side):
        rows = pl.ds(pl.multiple_of(i * 128, 128), 128)
        return pltpu.make_async_copy(so.at[side], (lnew, rnew)[side].at[rows], st_o.at[side])

    owner_of = [own[y, r] for r in range(14)]

    def row_of(d):
        row = jnp.int32(0)
        for r in range(14):
            row = jnp.where(owner_of[r] == d, jnp.int32(r), row)
        return row

    def line(ab, d):
        return ((x + d) % 4, z) if ab == 0 else (x, (z + d) % 4)

    def spread(src_of, mid, ab, d, send, recv):
        tx, tz = line(ab, d)
        here = x if ab == 0 else z
        return remote(src_of(ab, tx if ab == 0 else tz), mid.at[here], send, recv, device(tx, y, tz, core))

    def deliver(mid, dst_of, ab, d, dc, send, recv):
        tx, tz = line(1 - ab, d)
        tc = (core + dc) % 2
        return remote(mid.at[:, tz if ab == 0 else tx, tc], dst_of(ab), send, recv, device(tx, y, tz, tc))

    HOPS = [(d, dc) for d in (2, 1, 3, 0) for dc in (0, 1) if (d, dc) != (0, 0)]

    def owner_src(u):
        def src_of(ab, at):
            lanes = pl.ds(512 * ab, 512)
            return outb.at[at, :, :, u, :, lanes] if ab == 0 else outb.at[:, at, :, u, :, lanes]

        return src_of

    def owner_dst(u):
        def dst_of(ab):
            lanes = pl.ds(512 * ab, 512)
            return arr.at[:, z, core, u, :, lanes] if ab == 0 else arr.at[x, :, core, u, :, lanes]

        return dst_of

    def owner_spread(u):
        return [
            spread(owner_src(u), mid.at[u, ab], ab, d, o_s.at[u, ab, d], o_r.at[u, ab, d])
            for d in (2, 1, 3) for ab in (0, 1)
        ]

    def owner_deliver(u):
        return [
            deliver(mid.at[u, ab], owner_dst(u), ab, d, dc, q_s.at[u, ab, d, dc], q_r.at[u, ab, d, dc])
            for d, dc in HOPS for ab in (0, 1)
        ]

    def back_src(ab, at):
        return outb.at[at, :, :, 0] if ab == 0 else outb.at[:, at, :, 1]

    def back_dst(ab):
        return ret.at[:, z, core, 0] if ab == 0 else ret.at[x, :, core, 1]

    def back_spread(ab, d):
        return spread(back_src, midb.at[ab], ab, d, b_s.at[ab, d], b_r.at[ab, d])

    def back_tile(i, d):
        tx = lax.rem(x + 6 - i, 4)
        tz = (z + d) % 4
        return remote(outb.at[tx, tz, :, 1], midb.at[1, z, tx], t_s.at[i, d], t_r.at[i, d], device(x, y, tz, core))

    def back_deliver(ab, d, dc):
        return deliver(midb.at[ab], back_dst, ab, d, dc, c_s.at[ab, d, dc], c_r.at[ab, d, dc])

    passing = {}

    def send_owners(u):
        for s in range(4):
            for rel in (0, 1):
                if s == 0 and rel == 0:
                    y_cp[u, s, rel].wait()
                else:
                    y_cp[u, s, rel].wait_recv()
        for r in range(14):
            at = r * 1024
            done = 0
            while done < 1024:
                i, lane = (at + done) // PART, (at + done) % PART
                size = min(1024 - done, PART - lane)
                blocks[u, r, :, done : done + size] = sh[u, i, :, lane : lane + size]
                done += size

        @pl.loop(0, 32)
        def _(t):
            outb[t // 8, (t // 2) % 4, t % 2, u] = blocks[u, row_of(t)]

        passing[1, u] = owner_spread(u)
        for cp in passing[1, u]:
            go(cp)
        mid[u, 0, x] = outb[x, :, :, u, :, 0:512]
        mid[u, 1, z] = outb[:, z, :, u, :, 512:1024]

    def pass_owners(u):
        for cp in passing[1, u]:
            cp.wait_recv()
        passing[2, u] = owner_deliver(u)
        for cp in passing[2, u]:
            go(cp)
        arr[:, z, core, u, :, 0:512] = mid[u, 0, :, z, core]
        arr[x, :, core, u, :, 512:1024] = mid[u, 1, :, x, core]

    chunks = ((0, 0), (0, 1), (1, 0), (2, 0), (3, 0), (1, 1), (2, 1), (3, 1))
    for turn in range(12):
        for behind, stage in ((0, stage_a), (4, stage_e), (3, stage_d), (2, stage_c), (1, stage_b)):
            if 0 <= turn - behind < 8:
                stage(*chunks[turn - behind])
        if 1 <= turn <= 3:
            relay(turn)
        if turn == 1:
            along_y(3)
        if turn == 4:
            r_cp.wait()
            transpose_root(rt)
            l_root = pltpu.make_async_copy(lroot, tb, loc.at[3])
            l_root.start()
        if turn == 5:
            l_root.wait()
            transpose_root(lt)
            stat_in(0, 0).start()
            stat_in(0, 1).start()
        if turn == 9:
            send_owners(0)
    pass_owners(0)
    send_owners(1)
    pass_owners(1)
    mine = jnp.int32(0)
    for r in range(14):
        mine = jnp.where(owner_of[r] == me, jnp.int32(1), mine)
    for u in (0, 1):
        for cp in passing[2, u]:
            cp.wait_recv()
    for cp in sends:
        cp.wait_send()

    @pl.loop(0, 4)
    def _(i):
        g = lax.rem(6 - i, 4)
        tx = lax.rem(x + g, 4)
        rows = pl.ds(pl.multiple_of(tx * 256, 256), 256)
        inner = jnp.dot(
            rt[rows, :], arr[...].reshape(1024, 1024), preferred_element_type=F32
        ).astype(BF16)
        res = jnp.dot(inner, lt[...], preferred_element_type=F32).astype(BF16)
        outb[tx] = res.reshape(4, 2, 2, 16, 1024)
        for turn, d in ((0, 2), (1, 1), (3, 3)):

            @pl.when(i == turn)
            def _():
                back_spread(0, d).start()

        for d in (2, 1, 3):
            back_tile(i, d).start()

    midb[0, x] = outb[x, :, :, 0]
    midb[1, z] = outb[:, z, :, 1]

    @pl.loop(0, 8)
    def _(i):
        at = pl.ds(pl.multiple_of(i * 128, 128), 128)
        for w in range(4):
            tb[at, w * 256 : (w + 1) * 256] = jnp.transpose(arr[w, :, :, :, :, at].reshape(256, 128))

    def grams(first, last):
        @pl.loop(first, last)
        def _(i):
            rows = pl.ds(pl.multiple_of(i * 128, 128), 128)
            for side in (0, 1):
                if side == 0:
                    gram = jnp.dot(tb[rows, :], arr[...].reshape(1024, 1024), preferred_element_type=F32)
                else:
                    mine_rows = arr[i // 2, pl.ds(2 * (i % 2), 2)].reshape(128, 1024)
                    gram = jnp.dot(mine_rows, tb[...], preferred_element_type=F32)
                stat_in(i, side).wait()
                old = st[side]
                new = jnp.where(mine == 1, 0.9 * old + 0.1 * gram, old)

                @pl.when(i > 0)
                def _():
                    stat_out(i - 1, side).wait()

                so[side] = new
                stat_out(i, side).start()

                @pl.when(i < 7)
                def _():
                    stat_in(i + 1, side).start()

    grams(0, 4)
    for d in (2, 1, 3):
        back_spread(0, d).wait_recv()
        for i in range(4):
            back_tile(i, d).wait_recv()
    last = [back_deliver(ab, d, dc) for d, dc in HOPS for ab in (0, 1)]
    for cp in last:
        cp.start()
    ret[:, z, core, 0] = midb[0, :, z, core]
    ret[x, :, core, 1] = midb[1, :, x, core]
    grams(4, 8)
    for cp in last:
        cp.wait()
    for d in (2, 1, 3):
        back_spread(0, d).wait_send()
        for i in range(4):
            back_tile(i, d).wait_send()

    for r in range(14):
        update[0, :, r * 1024 : (r + 1) * 1024] = ret[
            owner_of[r] // 8, (owner_of[r] // 2) % 4, owner_of[r] % 2
        ].reshape(32, 1024)
    for side in (0, 1):
        stat_out(7, side).wait()


def step(emb, hid, eg, hg, cot, own, lstat, rstat, lroot, rroot):
    dma = pltpu.SemaphoreType.DMA
    vmem = pl.BlockSpec(memory_space=pltpu.VMEM)
    hbm = pl.BlockSpec(memory_space=pl.ANY)
    return pl.pallas_call(
        reduce_kernel,
        out_shape=(
            jax.ShapeDtypeStruct((1024, 1024), F32),
            jax.ShapeDtypeStruct((1024, 1024), F32),
            jax.ShapeDtypeStruct((1, 32, 2 * WIDTH), BF16),
        ),
        in_specs=[vmem] * 5 + [pl.BlockSpec(memory_space=pltpu.SMEM)] + [hbm] * 4,
        out_specs=(hbm, hbm, vmem),
        scratch_shapes=[
            pltpu.VMEM((4, 2, 4, 4, 64, 256), BF16),
            pltpu.VMEM((2, 256, PART), BF16),
            pltpu.VMEM((2, 4, 8, 256), F32),
            pltpu.VMEM((2, 8, 256), F32),
            pltpu.VMEM((2, 2, 4, 4, 4, 32, HALF), BF16),
            pltpu.VMEM((2, 2, 4, 6, 2, 32, HALF), BF16),
            pltpu.VMEM((2, 2, 4, 6, 16, HALF), BF16),
            pltpu.VMEM((2, 4, 2, 16, PART), BF16),
            pltpu.VMEM((2, 8, 16, PART), BF16),
            pltpu.VMEM((2, 14, 16, 1024), BF16),
            pltpu.VMEM((4, 4, 2, 2, 16, 1024), BF16),
            pltpu.VMEM((4, 4, 2, 2, 16, 1024), BF16),
            pltpu.VMEM((4, 4, 2, 2, 16, 1024), BF16),
            pltpu.VMEM((1024, 1024), BF16),
            pltpu.VMEM((1024, 1024), BF16),
            pltpu.VMEM((1024, 1024), BF16),
            pltpu.VMEM((2, 128, 1024), F32),
            pltpu.VMEM((2, 128, 1024), F32),
            pltpu.VMEM((2, 2, 4, 4, 2, 16, 512), BF16),
            pltpu.VMEM((2, 4, 4, 2, 16, 1024), BF16),
            dma((2, 4)), dma((2, 4)), dma((1,)), dma((1,)), dma((3,)), dma((3,)), dma((4,)), dma((4,)),
            dma((2, 2, 4, 6)), dma((2, 2, 4, 6)), dma((2, 2, 4, 6)), dma((2, 2, 4, 6)),
            dma((2, 4, 2)), dma((2, 4, 2)), dma((4,)),
            dma((2, 2, 4)), dma((2, 2, 4)), dma((2, 2, 4, 2)), dma((2, 2, 4, 2)),
            dma((2, 4)), dma((2, 4)), dma((2, 4, 2)), dma((2, 4, 2)), dma((4, 4)), dma((4, 4)),
            dma((2,)), dma((2,)),
        ],
        compiler_params=pltpu.CompilerParams(
            collective_id=0, has_side_effects=True, vmem_limit_bytes=62 * 2**20
        ),
        name="shampoo",
    )(emb, hid, eg, hg, cot, own, lstat, rstat, lroot, rroot)


def body(
    embedding,
    hidden,
    embed_gain,
    hidden_gain,
    cotangent,
    left_stat,
    right_stat,
    left_root,
    right_root,
    owners,
):
    return step(
        embedding, hidden, embed_gain, hidden_gain, cotangent, owners,
        left_stat, right_stat, left_root, right_root,
    )


def solution(mesh):
    placed = (
        P("dp", "mp"),
        P("dp", "mp"),
        P("mp"),
        P("mp"),
        P("dp", "mp"),
        P("dp", "mp"),
        P("dp", "mp"),
        P("dp", "mp"),
        P("dp", "mp"),
        P(),
    )
    return jax.shard_map(
        body,
        mesh=mesh,
        in_specs=placed,
        out_specs=(P("dp", "mp"), P("dp", "mp"), P("mp", "dp", None)),
        check_vma=False,
    )
```

```python
import functools

import jax
import jax.numpy as jnp
from jax import lax
from jax.experimental import pallas as pl
from jax.experimental.pallas import tpu as pltpu
from jax.sharding import PartitionSpec as P

MESH = pl.DeviceIdType.MESH
F32 = jnp.float32
BF16 = jnp.bfloat16
WIDTH = 7168
PART = 1792
HALF = 896
DELTAS = (0, 1, 3, 2)


def coords():
    dp = lax.axis_index("dp")
    return dp // 8, lax.axis_index("mp"), (dp // 2) % 4, dp % 2


def device(x, y, z, core):
    return ((x * 4 + z) * 2 + core, y)


def remote(src, dst, send, recv, dest):
    return pltpu.make_async_remote_copy(
        src_ref=src, dst_ref=dst, send_sem=send, recv_sem=recv, device_id=dest, device_id_type=MESH
    )


def row_squares(ref):
    acc = jnp.zeros((256, 128), F32)
    for i in range(PART // 128):
        v = ref[:, i * 128 : (i + 1) * 128].astype(F32)
        acc = acc + v * v
    return jnp.sum(jnp.transpose(acc), axis=0, keepdims=True)


def reduce_kernel(
    emb, hid, eg, hg, cot, own, lstat, rstat, lroot, rroot, lnew, rnew, update,
    ct, nb, sq, sc, part, r1, r2, yb, sh, blocks, outb, arr, ret, tb, rt, lt, st, so, mid, midb, rows_sm,
    sq_s, sq_r, sib_s, sib_r, ct_s, ct_r, rel_s, rel_r, p1_s, p1_r, p2_s, p2_r, y_s, y_r, loc,
    o_s, o_r, q_s, q_r, b_s, b_r, c_s, c_r, t_s, t_r, st_i, st_o,
):
    x, y, z, core = coords()
    sib = device(x, y, z, 1 - core)
    nbr = {
        "x": (device((x + 1) % 4, y, z, core), device((x + 3) % 4, y, z, core), x),
        "z": (device(x, y, (z + 1) % 4, core), device(x, y, (z + 3) % 4, core), z),
    }
    barrier = pltpu.get_barrier_semaphore()
    me = (x * 4 + z) * 2 + core

    for d in (1, 2, 3):
        for c in (core, 1 - core):
            pl.semaphore_signal(barrier, inc=1, device_id=device(x, (y + d) % 4, z, c), device_id_type=MESH)

    for peer in (sib, *nbr["x"][:2], *nbr["z"][:2]):
        pl.semaphore_signal(barrier, inc=1, device_id=peer, device_id_type=MESH)

    r_cp = pltpu.make_async_copy(rroot, tb, loc.at[2])
    r_cp.start()

    ct[0, core] = jnp.transpose(cot[...]).reshape(4, 4, 64, 256)
    sq[core, 0] = jnp.concatenate([row_squares(emb), row_squares(hid), jnp.zeros((6, 256), F32)], axis=0)

    @pl.when(core == 0)
    def _():
        nb[0] = emb[...]

    @pl.when(core == 1)
    def _():
        nb[1] = hid[...]

    pl.semaphore_wait(barrier, 11)

    sends = []

    def go(cp):
        cp.start()
        sends.append(cp)
        return cp

    sq_cp = [
        go(remote(sq.at[core, 0], sq.at[core, i], sq_s.at[rel, i], sq_r.at[rel, i],
                  device(x, (y + i) % 4, z, (core + rel) % 2)))
        for i in range(4) for rel in (0, 1) if (i, rel) != (0, 0)
    ]
    ct_cp = {}
    rel_cp = {}
    rel_cp[0] = go(remote(ct.at[0, core], ct.at[0, core], rel_s.at[0], rel_r.at[0], sib))

    def along_y(s):
        ct_cp[s] = go(
            remote(ct.at[0, core], ct.at[s, core], ct_s.at[s - 1], ct_r.at[s - 1],
                   device(x, (y + 4 - DELTAS[s]) % 4, z, core))
        )

    along_y(1)
    along_y(2)
    n_cp = remote(emb, nb.at[core], sib_s.at[0], sib_r.at[0], sib)

    @pl.when(core == 0)
    def _():
        remote(hid, nb.at[core], sib_s.at[0], sib_r.at[0], sib).start()

    @pl.when(core == 1)
    def _():
        remote(emb, nb.at[core], sib_s.at[0], sib_r.at[0], sib).start()

    sends.append(n_cp)
    gain = jnp.where(core == 0, eg[...], hg[...]).reshape(1, PART)
    for cp in sq_cp:
        cp.wait_recv()
    sc[...] = lax.rsqrt((sq[:, 0] + sq[:, 1] + sq[:, 2] + sq[:, 3]) / WIDTH + 1e-6)
    n_cp.wait_recv()
    rel_cp[0].wait_recv()
    scale = [jnp.where(core == 0, sc[t, 0:1], sc[t, 1:2]) for t in (0, 1)]

    def relay(s):
        ct_cp[s].wait_recv()
        rel_cp[s] = go(remote(ct.at[s, core], ct.at[s, core], rel_s.at[s], rel_r.at[s], sib))

    axes = (("x", "z"), ("z", "x"))
    cps = {}

    def ring1(ab, s, u, which=range(6)):
        plus, minus, pos = nbr[axes[ab][0]]
        p1, m1, m2 = (pos + 1) % 4, (pos + 3) % 4, (pos + 2) % 4
        src = part.at[ab, u, s]

        def cp(i, ref, dest):
            return remote(ref, r1.at[ab, u, s, i], p1_s.at[ab, u, s, i], p1_r.at[ab, u, s, i], dest)

        parts = (
            (m2, slice(0, 2), plus), (m2, slice(2, 4), minus),
            (p1, slice(2, 4), plus), (m1, slice(0, 2), minus),
            (p1, slice(0, 2), plus), (m1, slice(2, 4), minus),
        )
        return [cp(w, src.at[parts[w][0], parts[w][1]], parts[w][2]) for w in which], (pos, p1, m1)

    def ring2(ab, s, u):
        plus, minus, pos = nbr[axes[ab][1]]
        p1, m1, m2 = (pos + 1) % 4, (pos + 3) % 4, (pos + 2) % 4
        src = part.at[ab, u, s, nbr[axes[ab][0]][2]]

        def cp(i, ref, dest):
            return remote(ref, r2.at[ab, u, s, i], p2_s.at[ab, u, s, i], p2_r.at[ab, u, s, i], dest)

        return [
            cp(0, src.at[m2, 0:16], plus),
            cp(1, src.at[m2, 16:32], minus),
            cp(2, src.at[p1, 16:32], plus),
            cp(3, src.at[m1, 0:16], minus),
            cp(4, src.at[p1, 0:16], plus),
            cp(5, src.at[m1, 16:32], minus),
        ], (pos, p1, m1)

    def product(s):
        if s > 0:
            rel_cp[s].wait_recv()

        @pl.loop(0, 4)
        def _(i):
            g = lax.rem(6 - i, 4)
            xg = lax.rem(x + g, 4)
            zg = lax.rem(z + g, 4)

            def lhs(t, ab):
                v = ct[s, t, xg] if ab == 0 else ct[s, t, :, zg]
                return (v.reshape(256, 256).astype(F32) * scale[t]).astype(BF16)

            for ab, at in ((0, xg), (1, zg)):
                lanes = slice(ab * HALF, (ab + 1) * HALF)
                acc = jnp.dot(lhs(0, ab), nb[0, :, lanes], preferred_element_type=F32)
                acc = acc + jnp.dot(lhs(1, ab), nb[1, :, lanes], preferred_element_type=F32)
                res = acc.astype(BF16).reshape(4, 2, 2, 16, HALF)
                for u in (0, 1):
                    part[ab, u, s, at] = res[:, :, u].reshape(4, 32, HALF)

            for turn, which in ((0, (0, 1)), (1, (2,)), (3, (3,))):

                @pl.when(i == turn)
                def _():
                    for ab in (0, 1):
                        for c in ring1(ab, s, 0, which)[0]:
                            c.start()

    def add(a, *rest):
        out = a.astype(F32)
        for r in rest:
            out = out + r.astype(F32)
        return out

    def stage_a(s, u):
        if u == 0:
            product(s)
        for ab in (0, 1):
            cps[1, ab, s, u] = ring1(ab, s, u)
            for i in range(4):
                if u == 0:
                    sends.append(cps[1, ab, s, u][0][i])
                else:
                    go(cps[1, ab, s, u][0][i])

    def stage_b(s, u):
        for ab in (0, 1):
            c, (pos, p1, m1) = cps[1, ab, s, u]
            c[0].wait_recv()
            part[ab, u, s, p1, 0:2] = add(part[ab, u, s, p1, 0:2], r1[ab, u, s, 0]).astype(BF16)
            go(c[4])
            c[1].wait_recv()
            part[ab, u, s, m1, 2:4] = add(part[ab, u, s, m1, 2:4], r1[ab, u, s, 1]).astype(BF16)
            go(c[5])

    def stage_c(s, u):
        for ab in (0, 1):
            c, (pos, p1, m1) = cps[1, ab, s, u]
            for i in (2, 3, 4, 5):
                c[i].wait_recv()
            part[ab, u, s, pos, 0:2] = add(
                part[ab, u, s, pos, 0:2], r1[ab, u, s, 4], r1[ab, u, s, 3]
            ).astype(BF16)
            part[ab, u, s, pos, 2:4] = add(
                part[ab, u, s, pos, 2:4], r1[ab, u, s, 2], r1[ab, u, s, 5]
            ).astype(BF16)
            cps[2, ab, s, u] = ring2(ab, s, u)
            for i in range(4):
                go(cps[2, ab, s, u][0][i])

    def stage_d(s, u):
        for ab in (0, 1):
            c, (pos, p1, m1) = cps[2, ab, s, u]
            o = nbr[axes[ab][0]][2]
            c[0].wait_recv()
            part[ab, u, s, o, p1, 0:16] = add(part[ab, u, s, o, p1, 0:16], r2[ab, u, s, 0]).astype(BF16)
            go(c[4])
            c[1].wait_recv()
            part[ab, u, s, o, m1, 16:32] = add(part[ab, u, s, o, m1, 16:32], r2[ab, u, s, 1]).astype(BF16)
            go(c[5])

    y_cp = {}

    def stage_e(s, u):
        for ab in (0, 1):
            c, (pos, p1, m1) = cps[2, ab, s, u]
            o = nbr[axes[ab][0]][2]
            for i in (2, 3, 4, 5):
                c[i].wait_recv()
            lanes = slice(ab * HALF, (ab + 1) * HALF)
            g = gain[:, lanes]
            for to, more in ((0, (4, 3)), (1, (2, 5))):
                yb[u, s, to, :, lanes] = (
                    add(part[ab, u, s, o, pos, 16 * to : 16 * to + 16], *[r2[ab, u, s, m] for m in more]) * g
                ).astype(BF16)
        for rel in (0, 1):
            to = (core + rel) % 2
            if s == 0 and rel == 0:
                cp = pltpu.make_async_copy(yb.at[u, s, to], sh.at[u, core * 4 + y], loc.at[u])
                cp.start()
            else:
                cp = go(
                    remote(yb.at[u, s, to], sh.at[u, core * 4 + y], y_s.at[u, s, rel], y_r.at[u, s, rel],
                           device(x, (y + DELTAS[s]) % 4, z, to))
                )
            y_cp[u, s, rel] = cp

    def transpose_root(out):
        @pl.loop(0, 8)
        def _(i):
            at = pl.ds(pl.multiple_of(i * 128, 128), 128)
            out[at, :] = jnp.transpose(tb[:, at])

    def stat_in(i, side):
        rows = pl.ds(pl.multiple_of(i * 128, 128), 128)
        return pltpu.make_async_copy((lstat, rstat)[side].at[rows], st.at[side], st_i.at[side])

    def stat_out(i, side):
        rows = pl.ds(pl.multiple_of(i * 128, 128), 128)
        return pltpu.make_async_copy(so.at[side], (lnew, rnew)[side].at[rows], st_o.at[side])

    owner_of = [own[y, r] for r in range(14)]

    def row_of(d):
        row = jnp.int32(0)
        for r in range(14):
            row = jnp.where(owner_of[r] == d, jnp.int32(r), row)
        return row

    def line(ab, d):
        return ((x + d) % 4, z) if ab == 0 else (x, (z + d) % 4)

    def spread(src_of, mid, ab, d, send, recv):
        tx, tz = line(ab, d)
        here = x if ab == 0 else z
        return remote(src_of(ab, tx if ab == 0 else tz), mid.at[here], send, recv, device(tx, y, tz, core))

    def deliver(mid, dst_of, ab, d, dc, send, recv):
        tx, tz = line(1 - ab, d)
        tc = (core + dc) % 2
        return remote(mid.at[:, tz if ab == 0 else tx, tc], dst_of(ab), send, recv, device(tx, y, tz, tc))

    HOPS = [(d, dc) for d in (2, 1, 3, 0) for dc in (0, 1) if (d, dc) != (0, 0)]

    def owner_src(u):
        def src_of(ab, at):
            lanes = pl.ds(512 * ab, 512)
            return outb.at[at, :, :, u, :, lanes] if ab == 0 else outb.at[:, at, :, u, :, lanes]

        return src_of

    def owner_dst(u):
        def dst_of(ab):
            lanes = pl.ds(512 * ab, 512)
            return arr.at[:, z, core, u, :, lanes] if ab == 0 else arr.at[x, :, core, u, :, lanes]

        return dst_of

    def owner_spread(u):
        return [
            spread(owner_src(u), mid.at[u, ab], ab, d, o_s.at[u, ab, d], o_r.at[u, ab, d])
            for d in (2, 1, 3) for ab in (0, 1)
        ]

    def owner_deliver(u):
        return [
            deliver(mid.at[u, ab], owner_dst(u), ab, d, dc, q_s.at[u, ab, d, dc], q_r.at[u, ab, d, dc])
            for d, dc in HOPS for ab in (0, 1)
        ]

    def back_src(ab, at):
        return outb.at[at, :, :, 0] if ab == 0 else outb.at[:, at, :, 1]

    def back_dst(ab):
        return ret.at[:, z, core, 0] if ab == 0 else ret.at[x, :, core, 1]

    def back_spread(ab, d):
        return spread(back_src, midb.at[ab], ab, d, b_s.at[ab, d], b_r.at[ab, d])

    def back_tile(i, d):
        tx = lax.rem(x + 6 - i, 4)
        tz = (z + d) % 4
        return remote(outb.at[tx, tz, :, 1], midb.at[1, z, tx], t_s.at[i, d], t_r.at[i, d], device(x, y, tz, core))

    def back_deliver(ab, d, dc):
        return deliver(midb.at[ab], back_dst, ab, d, dc, c_s.at[ab, d, dc], c_r.at[ab, d, dc])

    passing = {}

    def send_owners(u):
        for s in range(4):
            for rel in (0, 1):
                if s == 0 and rel == 0:
                    y_cp[u, s, rel].wait()
                else:
                    y_cp[u, s, rel].wait_recv()
        for r in range(14):
            at = r * 1024
            done = 0
            while done < 1024:
                i, lane = (at + done) // PART, (at + done) % PART
                size = min(1024 - done, PART - lane)
                blocks[u, r, :, done : done + size] = sh[u, i, :, lane : lane + size]
                done += size

        @pl.loop(0, 32, unroll=8)
        def _(t):
            outb[t // 8, (t // 2) % 4, t % 2, u] = blocks[u, rows_sm[t]]

        passing[1, u] = owner_spread(u)
        for cp in passing[1, u]:
            go(cp)
        mid[u, 0, x] = outb[x, :, :, u, :, 0:512]
        mid[u, 1, z] = outb[:, z, :, u, :, 512:1024]

    def pass_owners(u):
        for cp in passing[1, u]:
            cp.wait_recv()
        passing[2, u] = owner_deliver(u)
        for cp in passing[2, u]:
            go(cp)
        arr[:, z, core, u, :, 0:512] = mid[u, 0, :, z, core]
        arr[x, :, core, u, :, 512:1024] = mid[u, 1, :, x, core]

    chunks = ((0, 0), (0, 1), (1, 0), (2, 0), (3, 0), (1, 1), (2, 1), (3, 1))
    for turn in range(12):
        for behind, stage in ((0, stage_a), (4, stage_e), (3, stage_d), (2, stage_c), (1, stage_b)):
            if 0 <= turn - behind < 8:
                stage(*chunks[turn - behind])
        if 1 <= turn <= 3:
            relay(turn)
        if turn == 1:
            along_y(3)
        if turn == 4:
            r_cp.wait()
            transpose_root(rt)
            l_root = pltpu.make_async_copy(lroot, tb, loc.at[3])
            l_root.start()
        if turn == 6:

            @pl.loop(0, 32)
            def _(t):
                rows_sm[t] = row_of(t)

        if turn == 5:
            l_root.wait()
            transpose_root(lt)
            stat_in(0, 0).start()
            stat_in(0, 1).start()
        if turn == 9:
            send_owners(0)
    pass_owners(0)
    send_owners(1)
    pass_owners(1)
    mine = jnp.int32(0)
    for r in range(14):
        mine = jnp.where(owner_of[r] == me, jnp.int32(1), mine)
    for u in (0, 1):
        for cp in passing[2, u]:
            cp.wait_recv()
    for cp in sends:
        cp.wait_send()

    @pl.loop(0, 4)
    def _(i):
        g = lax.rem(6 - i, 4)
        tx = lax.rem(x + g, 4)
        rows = pl.ds(pl.multiple_of(tx * 256, 256), 256)
        inner = jnp.dot(
            rt[rows, :], arr[...].reshape(1024, 1024), preferred_element_type=F32
        ).astype(BF16)
        res = jnp.dot(inner, lt[...], preferred_element_type=F32).astype(BF16)
        outb[tx] = res.reshape(4, 2, 2, 16, 1024)
        for turn, d in ((0, 2), (1, 1), (3, 3)):

            @pl.when(i == turn)
            def _():
                back_spread(0, d).start()

        for d in (2, 1, 3):
            back_tile(i, d).start()

    midb[0, x] = outb[x, :, :, 0]
    midb[1, z] = outb[:, z, :, 1]

    @pl.loop(0, 8)
    def _(i):
        at = pl.ds(pl.multiple_of(i * 128, 128), 128)
        for w in range(4):
            tb[at, w * 256 : (w + 1) * 256] = jnp.transpose(arr[w, :, :, :, :, at].reshape(256, 128))

    def grams(first, last):
        @pl.loop(first, last)
        def _(i):
            rows = pl.ds(pl.multiple_of(i * 128, 128), 128)
            for side in (0, 1):
                if side == 0:
                    gram = jnp.dot(tb[rows, :], arr[...].reshape(1024, 1024), preferred_element_type=F32)
                else:
                    mine_rows = arr[i // 2, pl.ds(2 * (i % 2), 2)].reshape(128, 1024)
                    gram = jnp.dot(mine_rows, tb[...], preferred_element_type=F32)
                stat_in(i, side).wait()
                old = st[side]
                new = jnp.where(mine == 1, 0.9 * old + 0.1 * gram, old)

                @pl.when(i > 0)
                def _():
                    stat_out(i - 1, side).wait()

                so[side] = new
                stat_out(i, side).start()

                @pl.when(i < 7)
                def _():
                    stat_in(i + 1, side).start()

    grams(0, 4)
    for d in (2, 1, 3):
        back_spread(0, d).wait_recv()
        for i in range(4):
            back_tile(i, d).wait_recv()
    last = [back_deliver(ab, d, dc) for d, dc in HOPS for ab in (0, 1)]
    for cp in last:
        cp.start()
    ret[:, z, core, 0] = midb[0, :, z, core]
    ret[x, :, core, 1] = midb[1, :, x, core]
    grams(4, 8)
    for cp in last:
        cp.wait()
    for d in (2, 1, 3):
        back_spread(0, d).wait_send()
        for i in range(4):
            back_tile(i, d).wait_send()

    for r in range(14):
        update[0, :, r * 1024 : (r + 1) * 1024] = ret[
            owner_of[r] // 8, (owner_of[r] // 2) % 4, owner_of[r] % 2
        ].reshape(32, 1024)
    for side in (0, 1):
        stat_out(7, side).wait()


def step(emb, hid, eg, hg, cot, own, lstat, rstat, lroot, rroot):
    dma = pltpu.SemaphoreType.DMA
    vmem = pl.BlockSpec(memory_space=pltpu.VMEM)
    hbm = pl.BlockSpec(memory_space=pl.ANY)
    return pl.pallas_call(
        reduce_kernel,
        out_shape=(
            jax.ShapeDtypeStruct((1024, 1024), F32),
            jax.ShapeDtypeStruct((1024, 1024), F32),
            jax.ShapeDtypeStruct((1, 32, 2 * WIDTH), BF16),
        ),
        in_specs=[vmem] * 5 + [pl.BlockSpec(memory_space=pltpu.SMEM)] + [hbm] * 4,
        out_specs=(hbm, hbm, vmem),
        scratch_shapes=[
            pltpu.VMEM((4, 2, 4, 4, 64, 256), BF16),
            pltpu.VMEM((2, 256, PART), BF16),
            pltpu.VMEM((2, 4, 8, 256), F32),
            pltpu.VMEM((2, 8, 256), F32),
            pltpu.VMEM((2, 2, 4, 4, 4, 32, HALF), BF16),
            pltpu.VMEM((2, 2, 4, 6, 2, 32, HALF), BF16),
            pltpu.VMEM((2, 2, 4, 6, 16, HALF), BF16),
            pltpu.VMEM((2, 4, 2, 16, PART), BF16),
            pltpu.VMEM((2, 8, 16, PART), BF16),
            pltpu.VMEM((2, 14, 16, 1024), BF16),
            pltpu.VMEM((4, 4, 2, 2, 16, 1024), BF16),
            pltpu.VMEM((4, 4, 2, 2, 16, 1024), BF16),
            pltpu.VMEM((4, 4, 2, 2, 16, 1024), BF16),
            pltpu.VMEM((1024, 1024), BF16),
            pltpu.VMEM((1024, 1024), BF16),
            pltpu.VMEM((1024, 1024), BF16),
            pltpu.VMEM((2, 128, 1024), F32),
            pltpu.VMEM((2, 128, 1024), F32),
            pltpu.VMEM((2, 2, 4, 4, 2, 16, 512), BF16),
            pltpu.VMEM((2, 4, 4, 2, 16, 1024), BF16),
            pltpu.SMEM((32,), jnp.int32),
            dma((2, 4)), dma((2, 4)), dma((1,)), dma((1,)), dma((3,)), dma((3,)), dma((4,)), dma((4,)),
            dma((2, 2, 4, 6)), dma((2, 2, 4, 6)), dma((2, 2, 4, 6)), dma((2, 2, 4, 6)),
            dma((2, 4, 2)), dma((2, 4, 2)), dma((4,)),
            dma((2, 2, 4)), dma((2, 2, 4)), dma((2, 2, 4, 2)), dma((2, 2, 4, 2)),
            dma((2, 4)), dma((2, 4)), dma((2, 4, 2)), dma((2, 4, 2)), dma((4, 4)), dma((4, 4)),
            dma((2,)), dma((2,)),
        ],
        compiler_params=pltpu.CompilerParams(
            collective_id=0, has_side_effects=True, vmem_limit_bytes=62 * 2**20
        ),
        name="shampoo",
    )(emb, hid, eg, hg, cot, own, lstat, rstat, lroot, rroot)


def body(
    embedding,
    hidden,
    embed_gain,
    hidden_gain,
    cotangent,
    left_stat,
    right_stat,
    left_root,
    right_root,
    owners,
):
    return step(
        embedding, hidden, embed_gain, hidden_gain, cotangent, owners,
        left_stat, right_stat, left_root, right_root,
    )


def solution(mesh):
    placed = (
        P("dp", "mp"),
        P("dp", "mp"),
        P("mp"),
        P("mp"),
        P("dp", "mp"),
        P("dp", "mp"),
        P("dp", "mp"),
        P("dp", "mp"),
        P("dp", "mp"),
        P(),
    )
    return jax.shard_map(
        body,
        mesh=mesh,
        in_specs=placed,
        out_specs=(P("dp", "mp"), P("dp", "mp"), P("mp", "dp", None)),
        check_vma=False,
    )
```
